128 devices in a mesh: pre: 32 (over z, x, core), exp: 4 (over y).
Axes of the slice: x: 4, y: 4, z: 4, core: 2. Of those that a mesh axis runs over, the one named last changes fastest.
Arguments:
- queries: bfloat16 [32, 8, 128, 576], P('pre', None, 'exp')
- draft_latents: bfloat16 [32, 8, 576], P('pre'), may hold values from -6 to 6
- prefix_latents: bfloat16 [8, 16384, 576], P(None, 'pre')
- prefix_of: int32 [32], replicated, may hold values from 0 to 7, as said below
- accepted: int32 [32], replicated, may hold values from 1 to 8
- w_uv: bfloat16 [128, 512, 128], P('exp'), may hold values from -1 to 1
- w_out: bfloat16 [16384, 7168], P('exp', 'pre'), may hold values from -0.1875 to 0.1875
- residual: bfloat16 [256, 7168], P(None, 'pre')
- norm_gain: bfloat16 [7168], P('pre'), may hold values from 0.5 to 1.5
- w_gate_up: bfloat16 [12, 7168, 2, 2048], P('exp', 'pre'), may hold values from -0.0625 to 0.0625
- w_down: bfloat16 [12, 2048, 7168], P('exp', None, 'pre'), may hold values from -0.125 to 0.125
- shared_gate_up: bfloat16 [7168, 2, 2048], P('pre', None, 'exp'), may hold values from -0.0625 to 0.0625
- shared_down: bfloat16 [2048, 7168], P('exp', 'pre'), may hold values from -0.125 to 0.125
- expert_ids: int32 [256, 8], replicated, may hold values from 0 to 11, all different within a row; in each aligned block of 256 rows (0 to 255, 256 to 511, ...) at most 192 rows name the same one
- expert_gates: float32 [256, 8], replicated, may hold values from 0.05 to 0.25
Outputs:
- layer_out: bfloat16 [256, 7168], P(None, 'pre')
The draws below stay inside these ranges and needn't reach their ends.
Inputs may be any that keep to these rules, and one draw needn't show every extreme that they name: `prefix_of`: every system prompt is named by some request. `expert_ids`: each expert is named by at most 192 of the 256 tokens, a bound that some block reaches.
All inputs are finite; a program needn't handle non-finite values.
Results may differ from the reference program's by a relative error of at most 0.01.
Values may be sent and summed in bfloat16 or wider, within the bound.
No kernel may reach another device: no remote copies, remote signals or barrier semaphores. Data moves between devices by JAX's collectives and lax.ppermute only.
A program may use at most 192 MiB of HBM per device.

```python
import math
import jax
import jax.numpy as jnp
import numpy as np
from jax import lax

D = 7168
H = 128
LAT = 512
ROPE = 64
HD = 128
FF = 2048
TOPK = 8
DRAFT = 8
PREFIXES = 8
PLEN = 16384
REQ = 32
TOKENS = 256
EXPERTS = 12
CAP = 192


def latent_rows(key):
    drawn = jax.random.normal(jax.random.fold_in(key, 11), (PREFIXES, PLEN, LAT + ROPE), jnp.float32)
    return drawn


def prefix_owners(key):
    shuffled = jax.random.permutation(jax.random.fold_in(key, 13), PREFIXES).astype(jnp.int32)
    others = jax.random.randint(jax.random.fold_in(key, 14), (REQ,), 0, PREFIXES).astype(jnp.int32)
    return jnp.concatenate([shuffled, others[PREFIXES:]])


def draw_prefix_latents(key, part):
    latents = latent_rows(key)
    return latents.astype(jnp.bfloat16)


def draw_prefix_of(key, part):
    return prefix_owners(key)


def draw_queries(key, part):
    key = jax.random.fold_in(key, 5)
    drawn = jax.random.normal(key, (REQ, DRAFT, H, LAT + ROPE), jnp.float32)
    return drawn.astype(jnp.bfloat16)


def draw_residual(key, part):
    key = jax.random.fold_in(key, 7)
    row_key, col_key, base_key = jax.random.split(key, 3)
    row_scale = 0.3 * jnp.exp(jnp.log(10.0) * jax.random.uniform(row_key, (TOKENS, 1), jnp.float32))
    col_scale = 3.0 ** (jnp.arange(D, dtype=jnp.float32) / D)[None, :] * jnp.exp(0.4 * (jax.random.uniform(col_key, (1, D), jnp.float32) - 0.5))
    drawn = jax.random.normal(base_key, (TOKENS, D), jnp.float32)
    return (drawn * row_scale * col_scale).astype(jnp.bfloat16)


def plant(result, rng, least, top_value):
    index_at = [jax.random.randint(jax.random.fold_in(rng, axis), (), 0, length) for axis, length in enumerate(result.shape)]
    widest = result.shape.index(max(result.shape))
    neighbour = index_at[:widest] + [(index_at[widest] + 1) % result.shape[widest]] + index_at[widest + 1:]
    return result.at[tuple(index_at)].set(least).at[tuple(neighbour)].set(top_value)


def steps_of(own_key, dims, cuts, low, largest):
    loudness, own = 1.0, jax.random.fold_in(own_key, 6)
    for axis_at, blocks in cuts:
        draws = jnp.exp(jax.random.uniform(jax.random.fold_in(own, axis_at), (blocks,), jnp.float32, low / len(cuts), largest / len(cuts)))
        loudness = loudness * jnp.repeat(draws, dims[axis_at] // blocks).reshape([-1 if axis == axis_at else 1 for axis in range(len(dims))])
    return loudness


def assign_block(key, own, number, rows, number_of, top, bound, slope):
    order = jax.random.permutation(key, number_of)
    crowded, usual = load_shares(number_of, rows * top, bound, slope, True), load_shares(number_of, rows * top, bound, slope, False)
    places = jnp.arange(number_of)

    def named(sizes, offset_by):
        used = int((sizes > 0).sum())
        fixed = max(1, used // 4)
        shifted = fixed + (places - fixed + offset_by * (used - fixed)) % max(1, number_of - fixed)
        return jnp.zeros((number_of,), jnp.int32).at[order[jnp.where(places < fixed, places, shifted)]].set(jnp.asarray(sizes, jnp.int32))

    sizes = jnp.where(number % 4 == 0, named(crowded, number // 4), named(usual, number - number // 4 - 1))
    mixed = jax.random.permutation(jax.random.fold_in(own, 3), number_of)
    donor, taker = mixed[0:number_of // 2 * 2:2], mixed[1:number_of // 2 * 2:2]
    room = jnp.minimum(sizes[donor] - 1, bound - sizes[taker]) // 2
    room = jnp.where((donor == order[0]) | (taker == order[0]) | (sizes[taker] == 0), 0, jnp.maximum(room, 0))
    shifted = jax.random.randint(jax.random.fold_in(own, 4), (number_of // 2,), 0, 1 << 20) % (room + 1)
    sizes = sizes.at[donor].add(-shifted).at[taker].add(shifted)
    labels = jnp.searchsorted(jnp.cumsum(sizes), jnp.arange(rows * top), side="right").astype(jnp.int32)
    grid = labels.reshape(top, rows).T
    grid = grid[jax.random.permutation(jax.random.fold_in(own, 1), rows)]
    offset_by = jax.random.randint(jax.random.fold_in(own, 2), (rows, 1), 0, top)
    return jnp.take_along_axis(grid, (jnp.arange(top)[None, :] + offset_by) % top, axis=1)


def load_shares(amount, total, limit, skew, full):
    portions = [(1 << 20) // math.isqrt(rank ** skew) + 1 for rank in range(1, amount + 1)]
    largest = limit if full else min(limit, max(-(-total // amount), total * portions[0] // sum(portions)))
    least = 1 if total - largest >= amount - 1 else 0
    given, rest = [largest] + [least] * (amount - 1), total - largest - least * (amount - 1)
    while rest > 0:
        movable = [i for i in range(1, amount) if given[i] < largest] or [i for i in range(1, amount) if given[i] < limit]
        mass, left = sum([portions[i] for i in movable]), rest
        for i in movable:
            more = min(limit - given[i], max(1, left * portions[i] // mass), rest)
            given[i] = given[i] + more
            rest = rest - more
    return np.array(given)


def gaussian(own_key, extent, width, most, shards=(), held_as=jnp.bfloat16):
    result = jax.random.normal(own_key, extent, jnp.float32) * width
    if len(shards) > 0:
        result = steps_of(own_key, extent, shards, -0.22, 0.18) * result
    return jnp.clip(result, min=-most, max=most).astype(held_as)


def setup_inputs(seed: int = 0) -> dict:
    streams_of = jax.random.split(jax.random.key(seed), 16)
    queries = draw_queries(jax.random.fold_in(streams_of[15], 71), 0)
    draft_latents = gaussian(streams_of[1], (REQ, DRAFT, LAT + ROPE), 1.0, 6.0, ((0, 32),))
    prefix_latents = draw_prefix_latents(jax.random.fold_in(streams_of[15], 71), 0)
    prefix_of = draw_prefix_of(jax.random.fold_in(streams_of[15], 71), 0)
    accepted = plant(jax.random.randint(streams_of[4], (REQ,), 1, DRAFT + 1), jax.random.fold_in(streams_of[4], 1), 1, DRAFT).astype(jnp.int32)
    w_uv = gaussian(streams_of[5], (H, LAT, HD), (LAT // 16) ** -0.5, 1.0, ((0, 4),))
    w_out = gaussian(streams_of[6], (H * HD, D), (H * HD // 16) ** -0.5, 0.1875, ((0, 4), (1, 32)))
    residual = draw_residual(jax.random.fold_in(streams_of[15], 71), 0)
    norm_gain = jnp.clip(1.0 + 0.1 * jax.random.normal(streams_of[8], (D,), jnp.float32), 0.5, 1.5).astype(jnp.bfloat16)
    w_gate_up = gaussian(streams_of[9], (EXPERTS, D, 2, FF), D ** -0.5, 0.0625, ((0, 4), (1, 32)))
    w_down = gaussian(streams_of[10], (EXPERTS, FF, D), FF ** -0.5, 0.125, ((0, 4), (2, 32)))
    shared_gate_up = gaussian(streams_of[11], (D, 2, FF), D ** -0.5, 0.0625, ((0, 32), (2, 4)))
    shared_down = gaussian(streams_of[12], (FF, D), FF ** -0.5, 0.125, ((0, 4), (1, 32)))
    expert_ids_keys = jax.random.split(jax.random.fold_in(streams_of[13], 1), TOKENS // TOKENS)
    expert_ids_turns = jax.random.permutation(jax.random.fold_in(streams_of[13], 3), TOKENS // TOKENS)
    expert_ids = jax.vmap(lambda own, number: assign_block(jax.random.fold_in(streams_of[13], 2), own, number, TOKENS, EXPERTS, TOPK, CAP, 2))(expert_ids_keys, expert_ids_turns).reshape((TOKENS, TOPK))
    expert_gates = jnp.clip(jax.random.uniform(streams_of[14], (TOKENS, TOPK), jnp.float32, 0.05, 0.25), 0.05, 0.25)
    return dict(queries=queries, draft_latents=draft_latents, prefix_latents=prefix_latents, prefix_of=prefix_of, accepted=accepted, w_uv=w_uv, w_out=w_out, residual=residual, norm_gain=norm_gain, w_gate_up=w_gate_up, w_down=w_down, shared_gate_up=shared_gate_up, shared_down=shared_down, expert_ids=expert_ids, expert_gates=expert_gates)


def silu_product(stacked):
    return jax.nn.silu(stacked[..., 0, :]) * stacked[..., 1, :]

def rounded(values):
    return lax.optimization_barrier(values.astype(jnp.bfloat16)).astype(jnp.float32)

def reference(queries, draft_latents, prefix_latents, prefix_of, accepted, w_uv, w_out, residual, norm_gain, w_gate_up, w_down, shared_gate_up, shared_down, expert_ids, expert_gates):
    softmax_scale = (HD + ROPE) ** (-0.5)
    up_table = w_uv.astype(jnp.float32)
    causal = jnp.arange(DRAFT)[None, :] <= jnp.arange(DRAFT)[:, None]

    def one_request(request):
        query_rows = queries[request].astype(jnp.float32)
        prefix_rows = lax.dynamic_index_in_dim(prefix_latents, prefix_of[request], 0, keepdims=False).astype(jnp.float32)
        drafts = draft_latents[request].astype(jnp.float32)
        far_scores = jnp.einsum('jhc,kc->jhk', query_rows, prefix_rows) * softmax_scale
        near_scores = jnp.einsum('jhc,ic->jhi', query_rows, drafts) * softmax_scale
        near_scores = jnp.where(causal[:, None, :], near_scores, -jnp.inf)
        row_top = jnp.maximum(lax.optimization_barrier(jnp.max(far_scores, -1)), lax.optimization_barrier(jnp.max(near_scores, -1)))
        far_weight = rounded(jnp.exp(far_scores - row_top[..., None]))
        near_weight = rounded(jnp.exp(near_scores - row_top[..., None]))
        weight_sum = lax.optimization_barrier(jnp.sum(far_weight, -1)) + lax.optimization_barrier(jnp.sum(near_weight, -1))
        summed = jnp.einsum('jhk,kc->jhc', far_weight, prefix_rows[:, :LAT]) + jnp.einsum('jhi,ic->jhc', near_weight, drafts[:, :LAT])
        context = summed / weight_sum[..., None]
        return jnp.einsum('jhc,hcv->jhv', context, up_table, precision=lax.Precision.HIGHEST).astype(jnp.bfloat16)
    head_out = lax.map(one_request, jnp.arange(REQ, dtype=jnp.int32)).reshape(TOKENS, H * HD)
    hidden = residual.astype(jnp.float32) + jnp.dot(head_out, w_out, preferred_element_type=jnp.float32)
    square = lax.optimization_barrier(jnp.mean(hidden * hidden, -1, keepdims=True))
    normed = (hidden * lax.rsqrt(square + 1e-06) * norm_gain.astype(jnp.float32)).astype(jnp.bfloat16)
    live = (jnp.arange(DRAFT)[None, :] < accepted[:, None]).reshape(TOKENS).astype(jnp.float32)

    def one_expert(running, expert):
        chosen = expert_ids == expert
        routed = jnp.any(chosen, -1)
        weights = lax.optimization_barrier(jnp.sum(jnp.where(chosen, expert_gates, 0.0), -1)) * live
        filled = jnp.sum(routed.astype(jnp.int32))
        row_index = jnp.nonzero(routed, size=CAP, fill_value=0)[0]
        in_use = (jnp.arange(CAP) < filled).astype(jnp.float32)
        inputs = normed[row_index]
        stacked = jnp.dot(inputs, w_gate_up[expert].reshape(D, 2 * FF), preferred_element_type=jnp.float32).reshape(CAP, 2, FF)
        activation = silu_product(stacked).astype(jnp.bfloat16)
        expert_out = jnp.dot(activation, w_down[expert], preferred_element_type=jnp.float32)
        return (running.at[row_index].add((weights[row_index] * in_use)[:, None] * expert_out), None)
    routed_sum, _ = lax.scan(one_expert, jnp.zeros((TOKENS, D), jnp.float32), jnp.arange(EXPERTS, dtype=jnp.int32))
    shared_pair = jnp.dot(normed, shared_gate_up.reshape(D, 2 * FF), preferred_element_type=jnp.float32).reshape(TOKENS, 2, FF)
    shared_act = silu_product(shared_pair).astype(jnp.bfloat16)
    shared_out = jnp.dot(shared_act, shared_down, preferred_element_type=jnp.float32)
    return (hidden + routed_sum + shared_out).astype(jnp.bfloat16)
```

```python
import functools
import math

import jax
import jax.numpy as jnp
from jax import lax
from jax.experimental import pallas as pl
from jax.experimental.pallas import tpu as pltpu
from jax.sharding import PartitionSpec as P

D = 7168
LAT = 512
ROPE = 64
HD = 128
DRAFT = 8
EXP_DEV = 3
CAP = 192
RING = 4
CHIPS = 16
HEADS = 32
ROWS = HEADS * DRAFT
MSG = ROWS + 16
PIECE = 656
ACT = 320
KEXP = (HD + ROPE) ** (-0.5) * math.log2(math.e)
BF = jnp.bfloat16
F32 = jnp.float32
VMEM_LIMIT = 56 * 1024 * 1024


def device_of(z, x, c):
    return (z * RING + x) * 2 + c


def pre_pairs(move):
    return [
        (device_of(z, x, c), device_of(*move(z, x, c)))
        for z in range(RING)
        for x in range(RING)
        for c in range(2)
    ]


CORE = pre_pairs(lambda z, x, c: (z, x, 1 - c))
X_BY = {d: pre_pairs(lambda z, x, c: (z, (x + d) % RING, c)) for d in (1, 2, 3)}
Z_BY = {d: pre_pairs(lambda z, x, c: ((z + d) % RING, x, c)) for d in (1, 2, 3)}
Y_BY = {d: [(e, (e + d) % RING) for e in range(RING)] for d in (1, 2, 3)}
SAME_CORE = [[chip * 2 + c for chip in range(CHIPS)] for c in range(2)]


def swap_core(value):
    return lax.ppermute(value, "pre", CORE)


def ring_gather(value, pairs):
    return [value] + [lax.ppermute(value, "pre", pairs[d]) for d in (1, 2, 3)]


def exp_sum(value):
    others = {d: lax.ppermute(value, "exp", Y_BY[d]).astype(F32) for d in (1, 2, 3)}
    return (value.astype(F32) + others[2]) + (others[1] + others[3])


def chip_exchange(value):
    return lax.all_to_all(value, "pre", 0, 0, axis_index_groups=SAME_CORE)


def dot(a, b, dims=((1,), (0,))):
    return lax.dot_general(a, b, (dims, ((), ())), preferred_element_type=F32)


def eye(n):
    return lax.broadcasted_iota(jnp.int32, (n, n), 0) == lax.broadcasted_iota(jnp.int32, (n, n), 1)


def column_to_rows(column):
    mask = eye(128)
    parts = [
        jnp.sum(jnp.where(mask, jnp.broadcast_to(column[b * 128 : (b + 1) * 128], (128, 128)), 0.0), 0, keepdims=True)
        for b in range(column.shape[0] // 128)
    ]
    return jnp.concatenate(parts, 0)


def three_terms(rows):
    high = rows.astype(BF).astype(F32)
    rest = rows - high
    mid = rest.astype(BF).astype(F32)
    return [high, mid, rest - mid]


def near_kernel(q_ref, k_ref, w_ref, out_ref, stat_ref, acc):
    keys = k_ref[...]
    scores = dot(q_ref[...], keys, ((1,), (1,)))
    draft = lax.broadcasted_iota(jnp.int32, scores.shape, 0) % DRAFT
    key = lax.broadcasted_iota(jnp.int32, scores.shape, 1)
    allowed = key <= draft
    top = jnp.max(jnp.where(allowed, scores, -jnp.inf), 1, keepdims=True)
    weight = jnp.where(allowed, jnp.exp2((scores - top) * KEXP), 0.0).astype(BF)
    total = jnp.sum(weight.astype(F32), 1, keepdims=True)
    acc[...] = dot(weight, keys[:, :LAT])
    stat_ref[...] = jnp.concatenate([column_to_rows(top), column_to_rows(total)], 0)
    for h in range(HEADS):
        rows = slice(h * DRAFT, (h + 1) * DRAFT)
        out_ref[rows, :] = dot(acc[rows, :].astype(BF), w_ref[h])


def far_kernel(prompt, place, q0_ref, q1_ref, la_ref, lb_ref, w_ref, out_ref, acc):
    i = pl.program_id(0)
    q = jnp.concatenate([q0_ref[0], q1_ref[0]], 0)
    la = la_ref[0]
    lb = lb_ref[0]
    sa = dot(q, la, ((1,), (1,)))
    sb = dot(q, lb, ((1,), (1,)))
    top = jnp.max(jnp.maximum(sa, sb), 1, keepdims=True)
    wa = jnp.exp2((sa - top) * KEXP).astype(BF)
    wb = jnp.exp2((sb - top) * KEXP).astype(BF)
    total = jnp.sum(wa.astype(F32) + wb.astype(F32), 1, keepdims=True)
    summed = dot(wa, la[:, :LAT]) + dot(wb, lb[:, :LAT])
    to = place[i]
    acc[:, to] = summed.reshape(HEADS, DRAFT, LAT)
    extra = three_terms(column_to_rows(top)) + three_terms(column_to_rows(total))
    out_ref[to, ROWS:MSG, :] = jnp.concatenate(extra + [jnp.zeros((4, 128), F32)], 0).astype(BF)

    @pl.when(i == CHIPS - 1)
    def _():
        for pair in range(HEADS // 2):
            both = [
                dot(acc[h].reshape(CHIPS * DRAFT, LAT).astype(BF), w_ref[h]).reshape(CHIPS, DRAFT, HD)
                for h in (2 * pair, 2 * pair + 1)
            ]
            out_ref[:, pair * 16 : (pair + 1) * 16, :] = jnp.concatenate(both, 1).astype(BF)


def combine_kernel(rec_ref, near_ref, stat_ref, out_ref):
    tops, totals = [], []
    for p in range(CHIPS):
        extra = rec_ref[p, ROWS:MSG, :].astype(F32)
        tops.append(extra[0:2] + extra[2:4] + extra[4:6])
        totals.append(extra[6:8] + extra[8:10] + extra[10:12])
    tops.append(stat_ref[0:2])
    totals.append(stat_ref[2:4])
    best = functools.reduce(jnp.maximum, tops)
    scale = [jnp.exp2((t - best) * KEXP) for t in tops]
    whole = functools.reduce(jnp.add, [s * t for s, t in zip(scale, totals)])
    scale = [s / whole for s in scale]
    blocks = []
    for b in range(2):
        table = jnp.concatenate(
            [s[b : b + 1] for s in scale] + [jnp.zeros((128 - len(scale), 128), F32)], 0
        ).T
        rows = slice(b * 128, (b + 1) * 128)
        value = near_ref[rows, :] * table[:, CHIPS : CHIPS + 1]
        for p in range(CHIPS):
            value = value + rec_ref[p, rows, :].astype(F32) * table[:, p : p + 1]
        blocks.append(value)
    value = jnp.concatenate(blocks, 0)
    flat = jnp.concatenate([value[h * DRAFT : (h + 1) * DRAFT] for h in range(HEADS)], 1).astype(BF)
    for p in range(CHIPS):
        out_ref[p] = flat


def interleave(core, own, other):
    n, width = own.shape
    own = own.reshape(CHIPS, 1, DRAFT, width)
    other = other.reshape(CHIPS, 1, DRAFT, width)
    first = jnp.where(core == 0, own, other)
    second = jnp.where(core == 0, other, own)
    return jnp.concatenate([first, second], 1).reshape(2 * n, width)


def gate_up_kernel(
    core_ref, own_ref, rcv_ref, gm_ref, go_ref, pick_ref, wm_ref, wo_ref, sm_ref, so_ref, out_ref, xm, xo
):
    e = pl.program_id(0)
    core = core_ref[0]

    @pl.when(e == 0)
    def _():
        hm = interleave(core, own_ref[0], rcv_ref[1])
        ho = interleave(core, own_ref[1], rcv_ref[0])
        square = jnp.sum(hm * hm, 1, keepdims=True) + jnp.sum(ho * ho, 1, keepdims=True)
        terms = three_terms(column_to_rows(square))
        rows = jnp.concatenate(terms + [jnp.zeros((10, 128), F32)], 0).astype(BF)
        xm[...] = (hm * gm_ref[...].astype(F32)).astype(BF)
        xo[...] = (ho * go_ref[...].astype(F32)).astype(BF)
        for i in range(CHIPS):
            out_ref[i, 640:656, :] = rows
        for g in range(2):
            pair = (dot(xm[...], sm_ref[g]) + dot(xo[...], so_ref[g])).astype(BF)
            for i in range(CHIPS):
                out_ref[i, 576 + g * 32 : 608 + g * 32, :] = pair[
                    (i % 8) * 32 : (i % 8 + 1) * 32, (i // 8) * 128 : (i // 8 + 1) * 128
                ]

    picked_m = dot(pick_ref[0], xm[...]).astype(BF)
    picked_o = dot(pick_ref[0], xo[...]).astype(BF)
    for g in range(2):
        pair = (dot(picked_m, wm_ref[g, 0]) + dot(picked_o, wo_ref[g, 0])).astype(BF)
        start = pl.multiple_of(g * 288 + e * 96, 16)
        for i in range(CHIPS):
            out_ref[i, pl.ds(start, 96), :] = pair[
                (i % 2) * 96 : (i % 2 + 1) * 96, (i // 2) * 128 : (i // 2 + 1) * 128
            ]


def act_kernel(rec_ref, pick_ref, out_ref, acc):
    i = pl.program_id(0)
    part = rec_ref[0].astype(F32)
    for p in range(1, 4):
        part = part + rec_ref[p].astype(F32)

    @pl.when(i == 0)
    def _():
        acc[...] = part

    @pl.when(i > 0)
    def _():
        acc[...] += part

    @pl.when(i == 3)
    def _():
        square = acc[640:642, :] + acc[642:644, :] + acc[644:646, :]
        inverse = lax.rsqrt(square / D + 1e-06)
        pick = pick_ref[...].astype(F32)
        factor = jnp.sum(pick[:, :128] * inverse[0:1] + pick[:, 128:] * inverse[1:2], 1, keepdims=True)
        gate = jnp.concatenate([acc[0:288, :], acc[576:608, :]], 0) * factor
        up = jnp.concatenate([acc[288:576, :], acc[608:640, :]], 0) * factor
        act = (jax.nn.silu(gate) * up).astype(BF)
        for p in range(CHIPS):
            out_ref[p] = act


def down_kernel(act_ref, wm_ref, wo_ref, sm_ref, so_ref, weight_ref, spread_ref, mine_ref, other_ref):
    pieces = []
    for e in range(EXP_DEV):
        rows = slice(e * 96, (e + 1) * 96)
        pieces.append(
            jnp.concatenate(
                [jnp.concatenate([act_ref[u * 2 + half, rows, :] for u in range(8)], 1) for half in range(2)], 0
            )
        )
    shared = jnp.concatenate(
        [jnp.concatenate([act_ref[u * 8 + t, 288:320, :] for u in range(2)], 1) for t in range(8)], 0
    )
    for w_ref, s_ref, out_ref in ((wm_ref, sm_ref, mine_ref), (wo_ref, so_ref, other_ref)):
        weighted = jnp.concatenate(
            [
                (dot(pieces[e], w_ref[e]) * weight_ref[e * CAP : (e + 1) * CAP, :]).astype(BF)
                for e in range(EXP_DEV)
            ],
            0,
        )
        total = dot(spread_ref[...], weighted) + dot(shared, s_ref[...])
        out_ref[...] = total.astype(out_ref.dtype)


def params(n=0):
    if n:
        return pltpu.CompilerParams(vmem_limit_bytes=VMEM_LIMIT, dimension_semantics=("arbitrary",) * n)
    return pltpu.CompilerParams(vmem_limit_bytes=VMEM_LIMIT)


def near_part(q, keys, w_uv):
    return pl.pallas_call(
        near_kernel,
        out_shape=(jax.ShapeDtypeStruct((ROWS, HD), F32), jax.ShapeDtypeStruct((4, 128), F32)),
        scratch_shapes=[pltpu.VMEM((ROWS, LAT), F32)],
        compiler_params=params(),
        name="near",
    )(q, keys, w_uv)


def far_part(prompt, place, q0, q1, la, lb, w_uv):
    width = LAT + ROPE
    positions = la.shape[1]
    latent = pl.BlockSpec((1, positions, width), lambda i, pr, to: (pr[i], 0, 0))
    return pl.pallas_call(
        far_kernel,
        out_shape=jax.ShapeDtypeStruct((CHIPS, MSG, HD), BF),
        grid_spec=pltpu.PrefetchScalarGridSpec(
            num_scalar_prefetch=2,
            grid=(CHIPS,),
            in_specs=[
                pl.BlockSpec((1, ROWS // 2, width), lambda i, pr, to: (i, 0, 0)),
                pl.BlockSpec((1, ROWS // 2, width), lambda i, pr, to: ((i % RING) * RING + i // RING, 0, 0)),
                latent,
                latent,
                pl.BlockSpec((HEADS, LAT, HD), lambda i, pr, to: (0, 0, 0)),
            ],
            out_specs=pl.BlockSpec((CHIPS, MSG, HD), lambda i, pr, to: (0, 0, 0)),
            scratch_shapes=[pltpu.VMEM((HEADS, CHIPS, DRAFT, LAT), F32)],
        ),
        compiler_params=params(1),
        name="far",
    )(prompt, place, q0, q1, la, lb, w_uv)


def combine(received, near_out, near_stat):
    return pl.pallas_call(
        combine_kernel,
        out_shape=jax.ShapeDtypeStruct((CHIPS, DRAFT, HEADS * HD), BF),
        compiler_params=params(),
        name="combine",
    )(received, near_out, near_stat)


def gate_up(core, own, rcv, gain_m, gain_o, pick, wm, wo, sm, so):
    width = own.shape[-1]
    half = wm.shape[-1]

    def whole(*shape):
        return pl.BlockSpec(shape, lambda e, c: (0,) * len(shape))

    weights = pl.BlockSpec((2, 1, width, half), lambda e, c: (0, e, 0, 0))
    return pl.pallas_call(
        gate_up_kernel,
        out_shape=jax.ShapeDtypeStruct((CHIPS, PIECE, 128), BF),
        grid_spec=pltpu.PrefetchScalarGridSpec(
            num_scalar_prefetch=1,
            grid=(EXP_DEV,),
            in_specs=[
                whole(*own.shape),
                whole(*rcv.shape),
                whole(1, width),
                whole(1, width),
                pl.BlockSpec((1, CAP, 256), lambda e, c: (e, 0, 0)),
                weights,
                weights,
                whole(*sm.shape),
                whole(*so.shape),
            ],
            out_specs=whole(CHIPS, PIECE, 128),
            scratch_shapes=[pltpu.VMEM((256, width), BF), pltpu.VMEM((256, width), BF)],
        ),
        compiler_params=params(1),
        name="gate_up",
    )(core, own, rcv, gain_m, gain_o, pick, wm, wo, sm, so)


def activate(received, pick):
    return pl.pallas_call(
        act_kernel,
        out_shape=jax.ShapeDtypeStruct((CHIPS, ACT, 128), BF),
        grid=(4,),
        in_specs=[
            pl.BlockSpec((4, PIECE, 128), lambda i: (i, 0, 0)),
            pl.BlockSpec((ACT, 256), lambda i: (0, 0)),
        ],
        out_specs=pl.BlockSpec((CHIPS, ACT, 128), lambda i: (0, 0, 0)),
        scratch_shapes=[pltpu.VMEM((PIECE, 128), F32)],
        compiler_params=params(1),
        name="activate",
    )(received, pick)


def down(acts, wm, wo, sm, so, weight, spread):
    width = wm.shape[-1]
    return pl.pallas_call(
        down_kernel,
        out_shape=(jax.ShapeDtypeStruct((256, width), F32), jax.ShapeDtypeStruct((256, width), BF)),
        compiler_params=params(),
        name="down",
    )(acts, wm, wo, sm, so, weight, spread)


def halves(value, core, axis):
    size = value.shape[axis] // 2
    mine = lax.dynamic_slice_in_dim(value, core * size, size, axis)
    other = lax.dynamic_slice_in_dim(value, (1 - core) * size, size, axis)
    return mine, other


def per_device(
    queries,
    draft_latents,
    prefix_latents,
    prefix_of,
    accepted,
    w_uv,
    w_out,
    residual,
    norm_gain,
    w_gate_up,
    w_down,
    shared_gate_up,
    shared_down,
    expert_ids,
    expert_gates,
):
    pre = lax.axis_index("pre")
    core, chip = pre % 2, pre // 2
    z, x = chip // RING, chip % RING
    tokens = expert_ids.shape[0]

    q_own = queries[0].transpose(1, 0, 2).reshape(ROWS, LAT + ROPE)
    first = jnp.stack(ring_gather(q_own[: ROWS // 2], X_BY))
    second = jnp.stack(ring_gather(q_own[ROWS // 2 :], Z_BY))
    q0 = jnp.concatenate(ring_gather(first, Z_BY))
    q1 = jnp.concatenate(ring_gather(second, X_BY))

    latents_other = swap_core(prefix_latents)
    w_out_other = swap_core(w_out)
    residual_other = swap_core(residual)
    gain_other = swap_core(norm_gain)
    pair_m, pair_send = halves(w_gate_up.transpose(2, 0, 1, 3), core, 3)
    pair_o = swap_core(pair_send)
    shared_m, shared_send = halves(shared_gate_up.transpose(1, 0, 2), core, 2)
    shared_o = swap_core(shared_send)
    down_m, down_send = halves(w_down, core, 1)
    down_o = swap_core(down_send)
    shared_down_m, shared_down_send = halves(shared_down, core, 0)
    shared_down_o = swap_core(shared_down_send)

    live = (jnp.arange(DRAFT)[None, :] < accepted[:, None]).reshape(tokens).astype(F32)
    local_experts = lax.axis_index("exp") * EXP_DEV + jnp.arange(EXP_DEV, dtype=jnp.int32)
    chosen = expert_ids[:, :, None] == local_experts[None, None, :]
    routed = jnp.any(chosen, 1)
    weights = jnp.sum(jnp.where(chosen, expert_gates[:, :, None], 0.0), 1) * live[:, None]
    position = jnp.cumsum(routed.astype(jnp.int32), 0) - 1
    slot_hit = routed.T[:, None, :] & (
        position.T[:, None, :] == jnp.arange(CAP, dtype=jnp.int32)[None, :, None]
    )
    pick = slot_hit.astype(BF)
    spread = slot_hit.reshape(EXP_DEV * CAP, tokens).T.astype(BF)
    slot_weight = jnp.sum(jnp.where(slot_hit, weights.T[:, None, :], 0.0), 2).reshape(EXP_DEV * CAP, 1)
    my_slots = lax.dynamic_slice_in_dim(pick, (chip % 2) * 96, 96, 1).reshape(288, tokens)
    my_tokens = (
        jnp.arange(tokens, dtype=jnp.int32)[None, :]
        == (chip % 8) * 32 + jnp.arange(32, dtype=jnp.int32)[:, None]
    ).astype(BF)
    my_pick = jnp.concatenate([my_slots, my_tokens], 0)

    near_keys = jnp.pad(draft_latents[0], ((0, 128 - DRAFT), (0, 0)))
    near_out, near_stat = near_part(q_own, near_keys, w_uv)

    step = jnp.arange(CHIPS, dtype=jnp.int32)
    place = ((z - step // RING) % RING) * RING + (x - step % RING) % RING
    prompt = jnp.take(prefix_of, place * 2 + core, axis=0)
    messages = far_part(prompt, place, q0, q1, prefix_latents, latents_other, w_uv)
    heads = combine(chip_exchange(messages), near_out, near_stat)
    head_out = chip_exchange(heads).reshape(CHIPS * DRAFT, HEADS * HD)

    attention = jnp.stack([dot(head_out, w_out), dot(head_out, w_out_other)]).astype(BF)

    def own_tokens(value):
        value = value.reshape(CHIPS, 2, DRAFT, value.shape[-1])
        return lax.dynamic_index_in_dim(value, core, 1, False).reshape(CHIPS * DRAFT, -1)

    skip = jnp.stack([own_tokens(residual), own_tokens(residual_other)]).astype(F32)
    hidden = skip + exp_sum(attention)
    hidden_rcv = swap_core(hidden)

    pieces = gate_up(
        core[None].astype(jnp.int32),
        hidden,
        hidden_rcv,
        norm_gain[None],
        gain_other[None],
        pick,
        pair_m,
        pair_o,
        shared_m,
        shared_o,
    )
    acts = activate(chip_exchange(pieces), my_pick)
    mine, other = down(
        chip_exchange(acts), down_m, down_o, shared_down_m, shared_down_o, slot_weight, spread
    )
    mixed = exp_sum((mine + swap_core(other).astype(F32)).astype(BF))
    return (interleave(core, hidden[0], hidden_rcv[1]) + mixed).astype(BF)


def solution(mesh):
    return jax.shard_map(
        per_device,
        mesh=mesh,
        in_specs=(
            P("pre", None, "exp", None),
            P("pre", None, None),
            P(None, "pre", None),
            P(),
            P(),
            P("exp", None, None),
            P("exp", "pre"),
            P(None, "pre"),
            P("pre"),
            P("exp", "pre", None, None),
            P("exp", None, "pre"),
            P("pre", None, "exp"),
            P("exp", "pre"),
            P(),
            P(),
        ),
        out_specs=P(None, "pre"),
        check_vma=False,
    )
```

```python
import functools
import math

import jax
import jax.numpy as jnp
from jax import lax
from jax.experimental import pallas as pl
from jax.experimental.pallas import tpu as pltpu
from jax.sharding import PartitionSpec as P

D = 7168
LAT = 512
ROPE = 64
HD = 128
DRAFT = 8
EXP_DEV = 3
CAP = 192
RING = 4
CHIPS = 16
HEADS = 32
ROWS = HEADS * DRAFT
MSG = ROWS + 16
HALF = ROWS // 2
WIDTH = LAT + ROPE
QROWS = HALF * WIDTH // 128
GATE = 336
UP = 320
ACT = 320
KEXP = (HD + ROPE) ** (-0.5) * math.log2(math.e)
BF = jnp.bfloat16
F32 = jnp.float32


def device_of(z, x, c):
    return (z * RING + x) * 2 + c


def pre_pairs(move):
    return [
        (device_of(z, x, c), device_of(*move(z, x, c)))
        for z in range(RING)
        for x in range(RING)
        for c in range(2)
    ]


CORE = pre_pairs(lambda z, x, c: (z, x, 1 - c))
X_BY = {d: pre_pairs(lambda z, x, c: (z, (x + d) % RING, c)) for d in (1, 2, 3)}
Z_BY = {d: pre_pairs(lambda z, x, c: ((z + d) % RING, x, c)) for d in (1, 2, 3)}
Y_BY = {d: [(e, (e + d) % RING) for e in range(RING)] for d in (1, 2, 3)}
NEAR_SPOTS = [(0, 0)] + [(dz, dx) for dz in (0, 1, 3) for dx in (0, 1, 3) if dz or dx]
FAR_SPOTS = [(dz, dx) for dz in range(RING) for dx in range(RING) if 2 in (dz, dx)]
SAME_CORE = [[chip * 2 + c for chip in range(CHIPS)] for c in range(2)]


def swap_core(value):
    return lax.ppermute(value, "pre", CORE)


def ring_send(values, pairs):
    return [lax.ppermute(value, "pre", pairs[d]) for d, value in zip((1, 2, 3), values)]


def exp_sum(value):
    others = {d: lax.ppermute(value, "exp", Y_BY[d]).astype(F32) for d in (2, 1, 3)}
    return (value.astype(F32) + others[2]) + (others[1] + others[3])


def chip_exchange(value):
    return lax.all_to_all(value, "pre", 0, 0, axis_index_groups=SAME_CORE)


def dot(a, b, dims=((1,), (0,))):
    return lax.dot_general(a, b, (dims, ((), ())), preferred_element_type=F32)


NT = ((1,), (1,))


def eye(n):
    return lax.broadcasted_iota(jnp.int32, (n, n), 0) == lax.broadcasted_iota(jnp.int32, (n, n), 1)


def column_to_rows(column):
    mask = eye(128)
    parts = [
        jnp.sum(jnp.where(mask, jnp.broadcast_to(column[b * 128 : (b + 1) * 128], (128, 128)), 0.0), 0, keepdims=True)
        for b in range(column.shape[0] // 128)
    ]
    return jnp.concatenate(parts, 0)


def three_terms(rows):
    high = rows.astype(BF).astype(F32)
    rest = rows - high
    mid = rest.astype(BF).astype(F32)
    return [high, mid, rest - mid]


def near_kernel(q_ref, k_ref, w_ref, out_ref, stat_ref, acc):
    keys = k_ref[...]
    scores = dot(q_ref[...], keys, NT)
    draft = lax.broadcasted_iota(jnp.int32, scores.shape, 0) % DRAFT
    key = lax.broadcasted_iota(jnp.int32, scores.shape, 1)
    allowed = key <= draft
    top = jnp.max(jnp.where(allowed, scores, -jnp.inf), 1, keepdims=True)
    weight = jnp.where(allowed, jnp.exp2((scores - top) * KEXP), 0.0).astype(BF)
    total = jnp.sum(weight.astype(F32), 1, keepdims=True)
    acc[...] = dot(weight, keys[:, :LAT])
    stat_ref[...] = jnp.concatenate([column_to_rows(top), column_to_rows(total)], 0)
    for h in range(HEADS):
        rows = slice(h * DRAFT, (h + 1) * DRAFT)
        out_ref[rows, :] = dot(acc[rows, :].astype(BF), w_ref[h])


SLOTS = CHIPS // 2


def attend(q_ref, la_ref, lb_ref, out_ref, stat_ref):
    parts = []
    for b in range(4):
        rows = slice(b * HALF, (b + 1) * HALF)
        parts.append(jnp.concatenate([q_ref[0, rows, :], q_ref[1, rows, :]], 0))
    ropes = [q_ref[half, 4 * HALF : QROWS, :] for half in range(2)]
    parts.append(jnp.concatenate([r[:, s : s + ROPE] for r in ropes for s in (0, ROPE)], 0))
    q = jnp.concatenate(parts, 1)
    sa = dot(q, la_ref[...])
    sb = dot(q, lb_ref[...])
    top = jnp.max(jnp.maximum(sa, sb), 1, keepdims=True)
    wa = jnp.exp2((sa - top) * KEXP).astype(BF)
    wb = jnp.exp2((sb - top) * KEXP).astype(BF)
    total = jnp.sum(wa.astype(F32) + wb.astype(F32), 1, keepdims=True)
    out_ref[...] = (dot(wa, la_ref[:LAT], NT) + dot(wb, lb_ref[:LAT], NT)).astype(BF)
    stat_ref[...] = jnp.concatenate(
        [column_to_rows(top), column_to_rows(total), jnp.zeros((4, 128), F32)], 0
    )


def attend_all(plan, prompt, sources, la_ref, lb_ref, q_ref, sems, out_ref, stat_ref):
    for n, spots in enumerate(plan):
        for half, (source, at) in enumerate(spots):
            pltpu.make_async_copy(sources[source].at[at], q_ref.at[n, half], sems.at[n, half]).start()

    @pl.loop(0, SLOTS // 2)
    def _(pair):
        for r in range(2):
            n = pair * 2 + r
            for half in range(2):
                pltpu.make_async_copy(sources[0].at[0], q_ref.at[n, half], sems.at[n, half]).wait()
            which = prompt[n]
            attend(q_ref.at[n], la_ref.at[which], lb_ref.at[which], out_ref.at[n], stat_ref.at[n])


def far_first_kernel(plan, prompt, *refs):
    sources = refs[: -6]
    la_ref, lb_ref, out_ref, stat_ref, q_ref, sems = refs[-6:]
    attend_all(plan, prompt, sources, la_ref, lb_ref, q_ref, sems, out_ref, stat_ref)


def far_second_kernel(plan, prompt, place, *refs):
    sources = refs[: -11]
    la_ref, lb_ref, w_ref, early_ref, early_stat, msg_ref, q_ref, acc, stat, sems, early_sem = refs[-11:]
    fetch = pltpu.make_async_copy(early_ref, acc.at[pl.ds(0, SLOTS)], early_sem)
    fetch.start()
    attend_all(
        plan,
        prompt,
        sources,
        la_ref,
        lb_ref,
        q_ref,
        sems,
        acc.at[pl.ds(SLOTS, SLOTS)],
        stat,
    )
    fetch.wait()
    for n in range(CHIPS):
        rows = early_stat[n] if n < SLOTS else stat[n - SLOTS]
        extra = three_terms(rows[0:2]) + three_terms(rows[2:4]) + [jnp.zeros((4, 128), F32)]
        msg_ref[place[n], ROWS:MSG, :] = jnp.concatenate(extra, 0).astype(BF)
    low = lax.broadcasted_iota(jnp.int32, (CHIPS * 16, HD), 0) % 16 < DRAFT

    @pl.loop(0, HEADS // 4)
    def _(quad):
        for r in range(2):
            pair = quad * 2 + r
            start = pl.multiple_of(pair * 16, 16)
            rows = acc[:, pl.ds(start, 16), :].reshape(CHIPS * 16, LAT)
            both = dot(rows, jnp.concatenate([w_ref[pair * 2], w_ref[pair * 2 + 1]], 1))
            picked = jnp.where(low, both[:, :HD], both[:, HD:]).astype(BF)
            for n in range(CHIPS):
                msg_ref[place[n], pl.ds(start, 16), :] = picked[n * 16 : (n + 1) * 16]


def combine_kernel(rec_ref, near_ref, stat_ref, out_ref):
    tops, totals = [], []
    for p in range(CHIPS):
        extra = rec_ref[p, ROWS:MSG, :].astype(F32)
        tops.append(extra[0:2] + extra[2:4] + extra[4:6])
        totals.append(extra[6:8] + extra[8:10] + extra[10:12])
    tops.append(stat_ref[0:2])
    totals.append(stat_ref[2:4])
    best = functools.reduce(jnp.maximum, tops)
    scale = [jnp.exp2((t - best) * KEXP) for t in tops]
    whole = functools.reduce(jnp.add, [s * t for s, t in zip(scale, totals)])
    scale = [s / whole for s in scale]
    blocks = []
    for b in range(2):
        table = jnp.concatenate(
            [s[b : b + 1] for s in scale] + [jnp.zeros((128 - len(scale), 128), F32)], 0
        ).T
        rows = slice(b * 128, (b + 1) * 128)
        value = near_ref[rows, :] * table[:, CHIPS : CHIPS + 1]
        for p in range(CHIPS):
            value = value + rec_ref[p, rows, :].astype(F32) * table[:, p : p + 1]
        blocks.append(value)
    value = jnp.concatenate(blocks, 0)
    flat = jnp.concatenate([value[h * DRAFT : (h + 1) * DRAFT] for h in range(HEADS)], 1).astype(BF)
    for p in range(CHIPS):
        out_ref[p] = flat


def project_kernel(head_ref, wm_ref, wo_ref, out_ref, acc):
    k = pl.program_id(0)
    head = head_ref[...]
    part = jnp.concatenate([dot(wm_ref[...], head, NT), dot(wo_ref[...], head, NT)], 0)

    @pl.when(k == 0)
    def _():
        acc[...] = part

    @pl.when(k > 0)
    def _():
        acc[...] += part

    @pl.when(k == pl.num_programs(0) - 1)
    def _():
        out_ref[...] = acc[...].astype(BF)


def gate_up_kernel(
    at_ref, own_ref, rcv_ref, gm_ref, go_ref, pick_ref, wm_ref, wo_ref, sm_ref, so_ref, *refs
):
    outs, (xm, xo, pair, wide) = refs[:8], refs[8:]
    e = pl.program_id(0)
    core, z, x = at_ref[0], at_ref[1], at_ref[2]
    n = xm.shape[0]

    def destinations():
        for dx in range(RING):
            for dz in range(RING):
                chip = lax.rem(z + dz, RING) * RING + lax.rem(x + dx, RING)
                yield (outs[dx].at[dz], outs[RING + dz].at[dx]), chip

    @pl.when(e == 0)
    def _():
        square = jnp.zeros((1, 256), F32)
        for keep, gain_ref, mine, theirs in ((xm, gm_ref, 0, n), (xo, go_ref, n, 0)):
            own = own_ref[mine : mine + n, :]
            rcv = rcv_ref[theirs : theirs + n, :]
            whole = jnp.concatenate([jnp.where(core == 0, own, rcv), jnp.where(core == 0, rcv, own)], 1)
            square = square + jnp.sum(whole * whole, 0, keepdims=True)
            keep[...] = (whole * gain_ref[...]).astype(BF)
        terms = three_terms(jnp.concatenate([square[:, :128], square[:, 128:]], 0))
        rows = jnp.concatenate(terms + [jnp.zeros((10, 128), F32)], 0).astype(BF)
        same = eye(256).astype(BF)
        all_m = dot(same, xm[...], NT).astype(BF)
        all_o = dot(same, xo[...], NT).astype(BF)
        for g in range(2):
            pair[g] = (dot(all_m, sm_ref[g]) + dot(all_o, so_ref[g])).astype(BF)
        for pieces, chip in destinations():
            pieces[0][320:336, :] = rows
            top = pl.multiple_of(lax.rem(chip, 8) * 32, 32)
            left = pl.multiple_of(lax.div(chip, 8) * 128, 128)
            for g in range(2):
                pieces[g][288:320, :] = pair[g, pl.ds(top, 32), pl.ds(left, 128)]

    picked_m = dot(pick_ref[0], xm[...], NT).astype(BF)
    picked_o = dot(pick_ref[0], xo[...], NT).astype(BF)
    for g in range(2):
        wide[g] = (dot(picked_m, wm_ref[g, 0]) + dot(picked_o, wo_ref[g, 0])).astype(BF)
    start = pl.multiple_of(e * 96, 32)
    for pieces, chip in destinations():
        top = pl.multiple_of(lax.rem(chip, 2) * 96, 32)
        left = pl.multiple_of(lax.div(chip, 2) * 128, 128)
        for g in range(2):
            pieces[g][pl.ds(start, 96), :] = wide[g, pl.ds(top, 96), pl.ds(left, 128)]


def fold_kernel(*refs):
    for k in range(RING):
        total = refs[0][k].astype(F32)
        for r in refs[1:RING]:
            total = total + r[k].astype(F32)
        refs[RING + k][...] = total.astype(BF)


def act_kernel(*refs):
    gates, ups, pick_ref, out_ref = refs[:RING], refs[RING : 2 * RING], refs[-2], refs[-1]

    def total(parts):
        return functools.reduce(jnp.add, [part[...].astype(F32) for part in parts])

    gate, up = total(gates), total(ups)
    square = gate[320:322] + gate[322:324] + gate[324:326]
    inverse = lax.rsqrt(square / D + 1e-06)
    pick = pick_ref[...].astype(F32)
    factor = jnp.sum(pick[:, :128] * inverse[0:1] + pick[:, 128:] * inverse[1:2], 1, keepdims=True)
    act = (jax.nn.silu(gate[:ACT] * factor) * (up * factor)).astype(BF)
    for p in range(CHIPS):
        out_ref[p] = act


def down_kernel(act_ref, wm_ref, wo_ref, sm_ref, so_ref, weight_ref, pick_ref, mine_ref, other_ref):
    pieces = []
    for e in range(EXP_DEV):
        rows = slice(e * 96, (e + 1) * 96)
        pieces.append(
            jnp.concatenate(
                [jnp.concatenate([act_ref[u * 2 + half, rows, :] for u in range(8)], 1) for half in range(2)], 0
            )
        )
    shared = jnp.concatenate(
        [jnp.concatenate([act_ref[u * 8 + t, 288:320, :] for u in range(2)], 1) for t in range(8)], 0
    )
    for w_ref, s_ref, out_ref in ((wm_ref, sm_ref, mine_ref), (wo_ref, so_ref, other_ref)):
        total = dot(s_ref[...], shared, NT)
        for e in range(EXP_DEV):
            weighted = (dot(w_ref[e], pieces[e], NT) * weight_ref[e]).astype(BF)
            total = total + dot(weighted, pick_ref[e])
        out_ref[...] = total.astype(out_ref.dtype)


def params(n=0, limit=24):
    size = limit * 1024 * 1024
    if n:
        return pltpu.CompilerParams(vmem_limit_bytes=size, dimension_semantics=("arbitrary",) * n)
    return pltpu.CompilerParams(vmem_limit_bytes=size)


def shape(*dims, dtype=BF):
    return jax.ShapeDtypeStruct(dims, dtype)


def whole(*dims):
    return pl.BlockSpec(dims, lambda *at: (0,) * len(dims))


def near_part(q, keys, w_uv):
    return pl.pallas_call(
        near_kernel,
        out_shape=(shape(ROWS, HD, dtype=F32), shape(4, 128, dtype=F32)),
        scratch_shapes=[pltpu.VMEM((ROWS, LAT), F32)],
        compiler_params=params(),
        name="near",
    )(q, keys, w_uv)


def vmem():
    return pl.BlockSpec(memory_space=pltpu.VMEM)


def far_cost():
    rows = SLOTS * ROWS
    return pl.CostEstimate(
        flops=2 * rows * 1024 * (WIDTH + LAT), bytes_accessed=24 * 1024 * 1024, transcendentals=rows * 1024
    )


def far_first(plan, prompt, sources, la, lb):
    return pl.pallas_call(
        functools.partial(far_first_kernel, plan),
        out_shape=(shape(SLOTS, ROWS, LAT), shape(SLOTS, 8, 128, dtype=F32)),
        in_specs=[pl.BlockSpec(memory_space=pltpu.SMEM)]
        + [pl.BlockSpec(memory_space=pl.ANY)] * len(sources)
        + [vmem(), vmem()],
        out_specs=(vmem(), vmem()),
        scratch_shapes=[
            pltpu.VMEM((SLOTS, 2, QROWS, 128), BF),
            pltpu.SemaphoreType.DMA((SLOTS, 2)),
        ],
        compiler_params=params(limit=26),
        cost_estimate=far_cost(),
        name="far_first",
    )(prompt, *sources, la, lb)


def far_second(plan, prompt, place, sources, la, lb, w_uv, early, early_stat):
    return pl.pallas_call(
        functools.partial(far_second_kernel, plan),
        out_shape=shape(CHIPS, MSG, HD),
        in_specs=[pl.BlockSpec(memory_space=pltpu.SMEM)] * 2
        + [pl.BlockSpec(memory_space=pl.ANY)] * len(sources)
        + [vmem(), vmem(), vmem(), pl.BlockSpec(memory_space=pl.ANY), vmem()],
        out_specs=vmem(),
        scratch_shapes=[
            pltpu.VMEM((SLOTS, 2, QROWS, 128), BF),
            pltpu.VMEM((CHIPS, ROWS, LAT), BF),
            pltpu.VMEM((SLOTS, 8, 128), F32),
            pltpu.SemaphoreType.DMA((SLOTS, 2)),
            pltpu.SemaphoreType.DMA,
        ],
        compiler_params=params(limit=36),
        cost_estimate=far_cost(),
        name="far_second",
    )(prompt, place, *sources, la, lb, w_uv, early, early_stat)


def combine(received, near_out, near_stat):
    return pl.pallas_call(
        combine_kernel,
        out_shape=shape(CHIPS, DRAFT, HEADS * HD),
        compiler_params=params(),
        name="combine",
    )(received, near_out, near_stat)


def project(head, wm, wo):
    n, depth = wm.shape
    step = depth // 4
    return pl.pallas_call(
        project_kernel,
        out_shape=shape(2 * n, head.shape[0]),
        grid=(4,),
        in_specs=[
            pl.BlockSpec((head.shape[0], step), lambda k: (0, k)),
            pl.BlockSpec((n, step), lambda k: (0, k)),
            pl.BlockSpec((n, step), lambda k: (0, k)),
        ],
        out_specs=whole(2 * n, head.shape[0]),
        scratch_shapes=[pltpu.VMEM((2 * n, head.shape[0]), F32)],
        compiler_params=params(1),
        name="project",
    )(head, wm, wo)


def gate_up(at, own, rcv, gain_m, gain_o, pick, wm, wo, sm, so):
    n, half = wm.shape[2:]
    weights = pl.BlockSpec((2, 1, n, half), lambda e, c: (0, e, 0, 0))
    return pl.pallas_call(
        gate_up_kernel,
        out_shape=[shape(RING, GATE, 128)] * RING + [shape(RING, UP, 128)] * RING,
        grid_spec=pltpu.PrefetchScalarGridSpec(
            num_scalar_prefetch=1,
            grid=(EXP_DEV,),
            in_specs=[
                whole(*own.shape),
                whole(*rcv.shape),
                whole(n, 1),
                whole(n, 1),
                pl.BlockSpec((1, CAP, 256), lambda e, c: (e, 0, 0)),
                weights,
                weights,
                whole(*sm.shape),
                whole(*so.shape),
            ],
            out_specs=[whole(RING, GATE, 128)] * RING + [whole(RING, UP, 128)] * RING,
            scratch_shapes=[
                pltpu.VMEM((n, 256), BF),
                pltpu.VMEM((n, 256), BF),
                pltpu.VMEM((2, 256, 256), BF),
                pltpu.VMEM((2, CAP, half), BF),
            ],
        ),
        compiler_params=params(1),
        name="gate_up",
    )(at, own, rcv, gain_m, gain_o, pick, wm, wo, sm, so)


def fold(parts):
    return pl.pallas_call(
        fold_kernel,
        out_shape=[shape(*parts[0].shape[1:])] * RING,
        compiler_params=params(),
        name="fold",
    )(*parts)


def activate(gates, ups, pick):
    return pl.pallas_call(
        act_kernel,
        out_shape=shape(CHIPS, ACT, 128),
        compiler_params=params(),
        name="activate",
    )(*gates, *ups, pick)


def down(acts, wm, wo, sm, so, weight, pick):
    n = wm.shape[1]
    return pl.pallas_call(
        down_kernel,
        out_shape=(shape(n, 256, dtype=F32), shape(n, 256)),
        compiler_params=params(),
        name="down",
    )(acts, wm, wo, sm, so, weight, pick)


def halves(value, core, axis):
    size = value.shape[axis] // 2
    mine = lax.dynamic_slice_in_dim(value, core * size, size, axis)
    other = lax.dynamic_slice_in_dim(value, (1 - core) * size, size, axis)
    return mine, other


def by_core(value):
    tail = value.shape[1:]
    return value.reshape(CHIPS, 2, DRAFT, *tail).swapaxes(0, 1).reshape(2 * CHIPS * DRAFT, *tail)


def query_message(q):
    latent = q[:, :LAT].reshape(HALF, 4, 128).swapaxes(0, 1).reshape(4 * HALF, 128)
    rope = q[:, LAT:].reshape(2, HALF // 2, ROPE).swapaxes(0, 1).reshape(HALF // 2, 2 * ROPE)
    return jnp.concatenate([latent, rope], 0)


def per_device(
    queries,
    draft_latents,
    prefix_latents,
    prefix_of,
    accepted,
    w_uv,
    w_out,
    residual,
    norm_gain,
    w_gate_up,
    w_down,
    shared_gate_up,
    shared_down,
    expert_ids,
    expert_gates,
):
    pre = lax.axis_index("pre")
    core, chip = pre % 2, pre // 2
    z, x = chip // RING, chip % RING
    tokens = expert_ids.shape[0]

    q_own = queries[0].swapaxes(0, 1).reshape(ROWS, WIDTH)
    q_first = query_message(q_own[:HALF])
    q_second = query_message(q_own[HALF:])
    latents = prefix_latents.swapaxes(1, 2)
    latents_other = swap_core(latents)
    first = jnp.stack([q_first] + ring_send([q_first] * 3, X_BY))
    second = jnp.stack([q_second] + ring_send([q_second] * 3, Z_BY))
    first_1, first_3 = [lax.ppermute(first, "pre", Z_BY[d]) for d in (1, 3)]
    second_1, second_3 = [lax.ppermute(second, "pre", X_BY[d]) for d in (1, 3)]
    (first, w_out, residual, norm_gain, w_gate_up, w_down, shared_gate_up, shared_down, draft_latents) = (
        lax.optimization_barrier(
            (first, w_out, residual, norm_gain, w_gate_up, w_down, shared_gate_up, shared_down, draft_latents)
        )
    )
    pair_m, pair_send = halves(w_gate_up.transpose(2, 0, 1, 3), core, 3)
    shared_m, shared_send = halves(shared_gate_up.swapaxes(0, 1), core, 2)
    down_m, down_send = halves(w_down.swapaxes(1, 2), core, 2)
    shared_down_m, shared_down_send = halves(shared_down.T, core, 1)
    token = jnp.arange(tokens, dtype=jnp.int32)
    order = by_core(token)
    to_order = (token[:, None] == order[None, :]).astype(BF)
    skip_m, skip_send = halves(dot(residual.T, to_order).astype(BF), core, 1)
    gain_m = norm_gain[:, None]
    w_out = w_out.T
    live = by_core((jnp.arange(DRAFT)[None, :] < accepted[:, None]).reshape(tokens).astype(F32))
    local_experts = lax.axis_index("exp") * EXP_DEV + jnp.arange(EXP_DEV, dtype=jnp.int32)
    chosen = by_core(expert_ids)[:, :, None] == local_experts[None, None, :]
    routed = jnp.any(chosen, 1)
    weights = jnp.sum(jnp.where(chosen, by_core(expert_gates)[:, :, None], 0.0), 1) * live[:, None]
    position = jnp.cumsum(routed.astype(jnp.int32), 0) - 1
    slot_hit = routed.T[:, None, :] & (
        position.T[:, None, :] == jnp.arange(CAP, dtype=jnp.int32)[None, :, None]
    )
    pick = slot_hit.astype(BF)
    slot_weight = jnp.sum(jnp.where(slot_hit, weights.T[:, None, :], 0.0), 2)[:, None, :]
    my_slots = lax.dynamic_slice_in_dim(pick, (chip % 2) * 96, 96, 1).reshape(288, tokens)
    my_tokens = (token[None, :] == (chip % 8) * 32 + jnp.arange(32, dtype=jnp.int32)[:, None]).astype(BF)
    my_pick = jnp.concatenate([my_slots, my_tokens], 0)

    near_keys = jnp.pad(draft_latents[0], ((0, 128 - DRAFT), (0, 0)))
    near_out, near_stat = near_part(q_own, near_keys, w_uv)

    prepared = (pair_m, shared_m, down_m, shared_down_m, slot_weight, skip_m, gain_m, pick, my_pick, near_out, near_stat)
    sends = (pair_send, shared_send, down_send, shared_down_send, skip_send, gain_m, w_out)
    (first_1, first_3, second_1, second_3, prepared, sends) = lax.optimization_barrier(
        (first_1, first_3, second_1, second_3, prepared, sends)
    )
    pair_m, shared_m, down_m, shared_down_m, slot_weight, skip_m, gain_m, pick, my_pick, near_out, near_stat = prepared
    first_2 = [lax.ppermute(first_1[:2], "pre", Z_BY[1]), lax.ppermute(first_3[2:], "pre", Z_BY[3])]
    second_2 = [lax.ppermute(second_1[:2], "pre", X_BY[1]), lax.ppermute(second_3[2:], "pre", X_BY[3])]
    pair_o, shared_o, down_o, shared_down_o, skip_o, gain_o, w_out_o = [swap_core(v) for v in sends]
    w_out = sends[-1]
    skip = jnp.concatenate([skip_m, skip_o], 0)
    gain_m, gain_o = gain_m.astype(F32), gain_o.astype(F32)

    sources = (first, first_1, first_3, second, second_1, second_3, *first_2, *second_2)
    early, late, early_plan, late_plan = [], [], [], []
    for dz, dx in NEAR_SPOTS + FAR_SPOTS:
        spots = tuple(
            (base + {0: 0, 1: 1, 3: 2}[slow], fast) if slow != 2 else (base_far + fast // 2, fast % 2)
            for base, base_far, slow, fast in ((0, 6, dz, dx), (3, 8, dx, dz))
        )
        if len(early) < SLOTS:
            early.append((dz, dx))
            early_plan.append(spots)
        else:
            late.append((dz, dx))
            late_plan.append(spots)

    def chips_of(spots):
        back = jnp.array(spots, jnp.int32)
        return ((z - back[:, 0]) % RING) * RING + (x - back[:, 1]) % RING

    early_chip, late_chip = chips_of(early), chips_of(late)
    early_out, early_stat = far_first(
        early_plan, jnp.take(prefix_of, early_chip * 2 + core, axis=0), sources[:6], latents, latents_other
    )
    messages = far_second(
        late_plan,
        jnp.take(prefix_of, late_chip * 2 + core, axis=0),
        jnp.concatenate([early_chip, late_chip]),
        sources,
        latents,
        latents_other,
        w_uv,
        early_out,
        early_stat,
    )
    heads = combine(chip_exchange(messages), near_out, near_stat)
    head_out = chip_exchange(heads).reshape(CHIPS * DRAFT, HEADS * HD)
    hidden = skip.astype(F32) + exp_sum(project(head_out, w_out, w_out_o))
    hidden_rcv = swap_core(hidden)

    at = jnp.stack([core, z, x]).astype(jnp.int32)
    parts = gate_up(at, hidden, hidden_rcv, gain_m, gain_o, pick, pair_m, pair_o, shared_m, shared_o)
    gates, ups = parts[:RING], parts[RING:]
    gates_in = ring_send(gates[1:], X_BY)
    ups_in = ring_send(ups[1:], Z_BY)
    gates = fold([gates[0]] + gates_in)
    gates_in = ring_send(gates[1:], Z_BY)
    ups = fold([ups[0]] + ups_in)
    ups_in = ring_send(ups[1:], X_BY)
    acts = activate([gates[0]] + gates_in, [ups[0]] + ups_in, my_pick)
    mine, other = down(
        chip_exchange(acts), down_m, down_o, shared_down_m, shared_down_o, slot_weight, pick
    )
    mixed = exp_sum((mine + swap_core(other).astype(F32)).astype(BF))

    n = mine.shape[0]
    kept, other_half = hidden[:n], hidden_rcv[n:]
    hidden_m = jnp.where(
        core == 0, jnp.concatenate([kept, other_half], 1), jnp.concatenate([other_half, kept], 1)
    )
    return dot((hidden_m + mixed).astype(BF), to_order, NT).astype(BF).T


def solution(mesh):
    return jax.shard_map(
        per_device,
        mesh=mesh,
        in_specs=(
            P("pre", None, "exp", None),
            P("pre", None, None),
            P(None, "pre", None),
            P(),
            P(),
            P("exp", None, None),
            P("exp", "pre"),
            P(None, "pre"),
            P("pre"),
            P("exp", "pre", None, None),
            P("exp", None, "pre"),
            P("pre", None, "exp"),
            P("exp", "pre"),
            P(),
            P(),
        ),
        out_specs=P(None, "pre"),
        check_vma=False,
    )
```

```python
import functools
import math

import jax
import jax.numpy as jnp
from jax import lax
from jax.experimental import pallas as pl
from jax.experimental.pallas import tpu as pltpu
from jax.sharding import PartitionSpec as P

D = 7168
LAT = 512
ROPE = 64
HD = 128
DRAFT = 8
EXP_DEV = 3
CAP = 192
RING = 4
CHIPS = 16
HEADS = 32
ROWS = HEADS * DRAFT
MSG = ROWS + 16
HALF = ROWS // 2
WIDTH = LAT + ROPE
QROWS = HALF * WIDTH // 128
GATE = 336
UP = 320
ACT = 320
KEXP = (HD + ROPE) ** (-0.5) * math.log2(math.e)
BF = jnp.bfloat16
F32 = jnp.float32


def device_of(z, x, c):
    return (z * RING + x) * 2 + c


def pre_pairs(move):
    return [
        (device_of(z, x, c), device_of(*move(z, x, c)))
        for z in range(RING)
        for x in range(RING)
        for c in range(2)
    ]


CORE = pre_pairs(lambda z, x, c: (z, x, 1 - c))
X_BY = {d: pre_pairs(lambda z, x, c: (z, (x + d) % RING, c)) for d in (1, 2, 3)}
Z_BY = {d: pre_pairs(lambda z, x, c: ((z + d) % RING, x, c)) for d in (1, 2, 3)}
Y_BY = {d: [(e, (e + d) % RING) for e in range(RING)] for d in (1, 2, 3)}
NEAR_SPOTS = [(0, 0)] + [(dz, dx) for dz in (0, 1, 3) for dx in (0, 1, 3) if dz or dx]
FAR_SPOTS = [(dz, dx) for dz in range(RING) for dx in range(RING) if 2 in (dz, dx)]
SAME_CORE = [[chip * 2 + c for chip in range(CHIPS)] for c in range(2)]


def swap_core(value):
    return lax.ppermute(value, "pre", CORE)


def ring_send(values, pairs):
    return [lax.ppermute(value, "pre", pairs[d]) for d, value in zip((1, 2, 3), values)]


def exp_sum(value):
    others = {d: lax.ppermute(value, "exp", Y_BY[d]).astype(F32) for d in (2, 1, 3)}
    return (value.astype(F32) + others[2]) + (others[1] + others[3])


def chip_exchange(value):
    return lax.all_to_all(value, "pre", 0, 0, axis_index_groups=SAME_CORE)


def dot(a, b, dims=((1,), (0,))):
    return lax.dot_general(a, b, (dims, ((), ())), preferred_element_type=F32)


NT = ((1,), (1,))


def eye(n):
    return lax.broadcasted_iota(jnp.int32, (n, n), 0) == lax.broadcasted_iota(jnp.int32, (n, n), 1)


def column_to_rows(column):
    mask = eye(128)
    parts = [
        jnp.sum(jnp.where(mask, jnp.broadcast_to(column[b * 128 : (b + 1) * 128], (128, 128)), 0.0), 0, keepdims=True)
        for b in range(column.shape[0] // 128)
    ]
    return jnp.concatenate(parts, 0)


def three_terms(rows):
    high = rows.astype(BF).astype(F32)
    rest = rows - high
    mid = rest.astype(BF).astype(F32)
    return [high, mid, rest - mid]


def near_kernel(q_ref, k_ref, w_ref, out_ref, stat_ref, acc):
    keys = k_ref[...]
    scores = dot(q_ref[...], keys, NT)
    draft = lax.broadcasted_iota(jnp.int32, scores.shape, 0) % DRAFT
    key = lax.broadcasted_iota(jnp.int32, scores.shape, 1)
    allowed = key <= draft
    top = jnp.max(jnp.where(allowed, scores, -jnp.inf), 1, keepdims=True)
    weight = jnp.where(allowed, jnp.exp2((scores - top) * KEXP), 0.0).astype(BF)
    total = jnp.sum(weight.astype(F32), 1, keepdims=True)
    acc[...] = dot(weight, keys[:, :LAT])
    stat_ref[...] = jnp.concatenate([column_to_rows(top), column_to_rows(total)], 0)
    for h in range(HEADS):
        rows = slice(h * DRAFT, (h + 1) * DRAFT)
        out_ref[rows, :] = dot(acc[rows, :].astype(BF), w_ref[h])


SLOTS = CHIPS // 2


def attend(q_refs, la_ref, lb_ref, out_ref, stat_ref):
    parts = []
    for b in range(4):
        rows = slice(b * HALF, (b + 1) * HALF)
        parts.append(jnp.concatenate([q[rows, :] for q in q_refs], 0))
    ropes = [q[4 * HALF : QROWS, :] for q in q_refs]
    parts.append(jnp.concatenate([r[:, s : s + ROPE] for r in ropes for s in (0, ROPE)], 0))
    q = jnp.concatenate(parts, 1)
    sa = dot(q, la_ref[...])
    sb = dot(q, lb_ref[...])
    top = jnp.max(jnp.maximum(sa, sb), 1, keepdims=True)
    wa = jnp.exp2((sa - top) * KEXP).astype(BF)
    wb = jnp.exp2((sb - top) * KEXP).astype(BF)
    total = jnp.sum(wa.astype(F32) + wb.astype(F32), 1, keepdims=True)
    out_ref[...] = (dot(wa, la_ref[:LAT], NT) + dot(wb, lb_ref[:LAT], NT)).astype(BF)
    stat_ref[...] = jnp.concatenate(
        [column_to_rows(top), column_to_rows(total), jnp.zeros((4, 128), F32)], 0
    )


def attend_all(plan, prompt, sources, la_ref, lb_ref, out_ref, stat_ref):
    for n, spots in enumerate(plan):
        which = prompt[n]
        q_refs = [sources[source].at[at] for source, at in spots]
        attend(q_refs, la_ref.at[which], lb_ref.at[which], out_ref.at[n], stat_ref.at[n])


def far_first_kernel(plan, prompt, *refs):
    attend_all(plan, prompt, refs[:-4], *refs[-4:])


def far_second_kernel(plan, prompt, place, *refs):
    sources = refs[:-9]
    la_ref, lb_ref, w_ref, early_ref, early_stat, msg_ref, acc, stat, early_sem = refs[-9:]
    fetch = pltpu.make_async_copy(early_ref, acc.at[pl.ds(0, SLOTS)], early_sem)
    fetch.start()
    attend_all(plan, prompt, sources, la_ref, lb_ref, acc.at[pl.ds(SLOTS, SLOTS)], stat)
    fetch.wait()
    for n in range(CHIPS):
        rows = early_stat[n] if n < SLOTS else stat[n - SLOTS]
        extra = three_terms(rows[0:2]) + three_terms(rows[2:4]) + [jnp.zeros((4, 128), F32)]
        msg_ref[place[n], ROWS:MSG, :] = jnp.concatenate(extra, 0).astype(BF)
    low = lax.broadcasted_iota(jnp.int32, (CHIPS * 16, HD), 0) % 16 < DRAFT

    @pl.loop(0, HEADS // 4)
    def _(quad):
        for r in range(2):
            pair = quad * 2 + r
            start = pl.multiple_of(pair * 16, 16)
            rows = acc[:, pl.ds(start, 16), :].reshape(CHIPS * 16, LAT)
            both = dot(rows, jnp.concatenate([w_ref[pair * 2], w_ref[pair * 2 + 1]], 1))
            picked = jnp.where(low, both[:, :HD], both[:, HD:]).astype(BF)
            for n in range(CHIPS):
                msg_ref[place[n], pl.ds(start, 16), :] = picked[n * 16 : (n + 1) * 16]


def combine_kernel(rec_ref, near_ref, stat_ref, out_ref):
    tops, totals = [], []
    for p in range(CHIPS):
        extra = rec_ref[p, ROWS:MSG, :].astype(F32)
        tops.append(extra[0:2] + extra[2:4] + extra[4:6])
        totals.append(extra[6:8] + extra[8:10] + extra[10:12])
    tops.append(stat_ref[0:2])
    totals.append(stat_ref[2:4])
    best = functools.reduce(jnp.maximum, tops)
    scale = [jnp.exp2((t - best) * KEXP) for t in tops]
    whole = functools.reduce(jnp.add, [s * t for s, t in zip(scale, totals)])
    scale = [s / whole for s in scale]
    blocks = []
    for b in range(2):
        table = jnp.concatenate(
            [s[b : b + 1] for s in scale] + [jnp.zeros((128 - len(scale), 128), F32)], 0
        ).T
        rows = slice(b * 128, (b + 1) * 128)
        value = near_ref[rows, :] * table[:, CHIPS : CHIPS + 1]
        for p in range(CHIPS):
            value = value + rec_ref[p, rows, :].astype(F32) * table[:, p : p + 1]
        blocks.append(value)
    value = jnp.concatenate(blocks, 0)
    flat = jnp.concatenate([value[h * DRAFT : (h + 1) * DRAFT] for h in range(HEADS)], 1).astype(BF)
    for p in range(CHIPS):
        out_ref[p] = flat


def project_kernel(head_ref, wm_ref, wo_ref, out_ref, acc):
    k = pl.program_id(0)
    head = head_ref[...]
    part = jnp.concatenate([dot(wm_ref[...], head, NT), dot(wo_ref[...], head, NT)], 0)

    @pl.when(k == 0)
    def _():
        acc[...] = part

    @pl.when(k > 0)
    def _():
        acc[...] += part

    @pl.when(k == pl.num_programs(0) - 1)
    def _():
        out_ref[...] = acc[...].astype(BF)


def gate_up_kernel(
    at_ref, own_ref, rcv_ref, pick_ref, wm_ref, wo_ref, sm_ref, so_ref, *refs
):
    outs, (xm, xo, pair, wide) = refs[:8], refs[8:]
    e = pl.program_id(0)
    core, z, x = at_ref[0], at_ref[1], at_ref[2]
    n = xm.shape[0]

    def destinations():
        for dx in range(RING):
            for dz in range(RING):
                chip = lax.rem(z + dz, RING) * RING + lax.rem(x + dx, RING)
                yield (outs[dx].at[dz], outs[RING + dz].at[dx]), chip

    @pl.when(e == 0)
    def _():
        square = jnp.zeros((1, 256), F32)
        for keep, misc_ref, mine, theirs in ((xm, sm_ref, 0, n), (xo, so_ref, n, 0)):
            own = own_ref[mine : mine + n, :]
            rcv = rcv_ref[theirs : theirs + n, :]
            whole = jnp.concatenate([jnp.where(core == 0, own, rcv), jnp.where(core == 0, rcv, own)], 1)
            square = square + jnp.sum(whole * whole, 0, keepdims=True)
            keep[...] = (whole * misc_ref[3][:, 128:129].astype(F32)).astype(BF)
        terms = three_terms(jnp.concatenate([square[:, :128], square[:, 128:]], 0))
        rows = jnp.concatenate(terms + [jnp.zeros((10, 128), F32)], 0).astype(BF)
        same = eye(256).astype(BF)
        all_m = dot(same, xm[...], NT).astype(BF)
        all_o = dot(same, xo[...], NT).astype(BF)
        for g in range(2):
            pair[g] = (dot(all_m, sm_ref[g]) + dot(all_o, so_ref[g])).astype(BF)
        for pieces, chip in destinations():
            pieces[0][320:336, :] = rows
            top = pl.multiple_of(lax.rem(chip, 8) * 32, 32)
            left = pl.multiple_of(lax.div(chip, 8) * 128, 128)
            for g in range(2):
                pieces[g][288:320, :] = pair[g, pl.ds(top, 32), pl.ds(left, 128)]

    picked_m = dot(pick_ref[0], xm[...], NT).astype(BF)
    picked_o = dot(pick_ref[0], xo[...], NT).astype(BF)
    for g in range(2):
        wide[g] = (dot(picked_m, wm_ref[g, 0]) + dot(picked_o, wo_ref[g, 0])).astype(BF)
    start = pl.multiple_of(e * 96, 32)
    for pieces, chip in destinations():
        top = pl.multiple_of(lax.rem(chip, 2) * 96, 32)
        left = pl.multiple_of(lax.div(chip, 2) * 128, 128)
        for g in range(2):
            pieces[g][pl.ds(start, 96), :] = wide[g, pl.ds(top, 96), pl.ds(left, 128)]


def fold_kernel(*refs):
    for k in range(RING):
        total = refs[0][k].astype(F32)
        for r in refs[1:RING]:
            total = total + r[k].astype(F32)
        refs[RING + k][...] = total.astype(BF)


def act_kernel(*refs):
    gates, ups, pick_ref, out_ref = refs[:RING], refs[RING : 2 * RING], refs[-2], refs[-1]

    def total(parts):
        return functools.reduce(jnp.add, [part[...].astype(F32) for part in parts])

    gate, up = total(gates), total(ups)
    square = gate[320:322] + gate[322:324] + gate[324:326]
    inverse = lax.rsqrt(square / D + 1e-06)
    pick = pick_ref[...].astype(F32)
    factor = jnp.sum(pick[:, :128] * inverse[0:1] + pick[:, 128:] * inverse[1:2], 1, keepdims=True)
    act = (jax.nn.silu(gate[:ACT] * factor) * (up * factor)).astype(BF)
    for p in range(CHIPS):
        out_ref[p] = act


def down_kernel(act_ref, wm_ref, wo_ref, sm_ref, so_ref, weight_ref, pick_ref, mine_ref, other_ref):
    pieces = []
    for e in range(EXP_DEV):
        rows = slice(e * 96, (e + 1) * 96)
        pieces.append(
            jnp.concatenate(
                [jnp.concatenate([act_ref[u * 2 + half, rows, :] for u in range(8)], 1) for half in range(2)], 0
            )
        )
    shared = jnp.concatenate(
        [jnp.concatenate([act_ref[u * 8 + t, 288:320, :] for u in range(2)], 1) for t in range(8)], 0
    )
    for w_ref, s_ref, out_ref in ((wm_ref, sm_ref, mine_ref), (wo_ref, so_ref, other_ref)):
        total = dot(s_ref[2], shared, NT)
        for e in range(EXP_DEV):
            weighted = (dot(w_ref[e], pieces[e], NT) * weight_ref[e]).astype(BF)
            total = total + dot(weighted, pick_ref[e])
        out_ref[...] = total.astype(out_ref.dtype)


def params(n=0, limit=24):
    size = limit * 1024 * 1024
    if n:
        return pltpu.CompilerParams(vmem_limit_bytes=size, dimension_semantics=("arbitrary",) * n)
    return pltpu.CompilerParams(vmem_limit_bytes=size)


def shape(*dims, dtype=BF):
    return jax.ShapeDtypeStruct(dims, dtype)


def whole(*dims):
    return pl.BlockSpec(dims, lambda *at: (0,) * len(dims))


def near_part(q, keys, w_uv):
    return pl.pallas_call(
        near_kernel,
        out_shape=(shape(ROWS, HD, dtype=F32), shape(4, 128, dtype=F32)),
        scratch_shapes=[pltpu.VMEM((ROWS, LAT), F32)],
        compiler_params=params(),
        name="near",
    )(q, keys, w_uv)


def vmem():
    return pl.BlockSpec(memory_space=pltpu.VMEM)


def far_cost():
    rows = SLOTS * ROWS
    return pl.CostEstimate(
        flops=2 * rows * 1024 * (WIDTH + LAT), bytes_accessed=24 * 1024 * 1024, transcendentals=rows * 1024
    )


def far_first(plan, prompt, sources, la, lb):
    return pl.pallas_call(
        functools.partial(far_first_kernel, plan),
        out_shape=(shape(SLOTS, ROWS, LAT), shape(SLOTS, 8, 128, dtype=F32)),
        in_specs=[pl.BlockSpec(memory_space=pltpu.SMEM)]
        + [vmem()] * len(sources)
        + [vmem(), vmem()],
        out_specs=(vmem(), vmem()),
        compiler_params=params(limit=18),
        cost_estimate=far_cost(),
        name="far_first",
    )(prompt, *sources, la, lb)


def far_second(plan, prompt, place, sources, la, lb, w_uv, early, early_stat):
    return pl.pallas_call(
        functools.partial(far_second_kernel, plan),
        out_shape=shape(CHIPS, MSG, HD),
        in_specs=[pl.BlockSpec(memory_space=pltpu.SMEM)] * 2
        + [vmem()] * len(sources)
        + [vmem(), vmem(), vmem(), pl.BlockSpec(memory_space=pl.ANY), vmem()],
        out_specs=vmem(),
        scratch_shapes=[
            pltpu.VMEM((CHIPS, ROWS, LAT), BF),
            pltpu.VMEM((SLOTS, 8, 128), F32),
            pltpu.SemaphoreType.DMA,
        ],
        compiler_params=params(limit=24),
        cost_estimate=far_cost(),
        name="far_second",
    )(prompt, place, *sources, la, lb, w_uv, early, early_stat)


def combine(received, near_out, near_stat):
    return pl.pallas_call(
        combine_kernel,
        out_shape=shape(CHIPS, DRAFT, HEADS * HD),
        compiler_params=params(),
        name="combine",
    )(received, near_out, near_stat)


def project(head, wm, wo):
    n, depth = wm.shape
    step = depth // 4
    return pl.pallas_call(
        project_kernel,
        out_shape=shape(2 * n, head.shape[0]),
        grid=(4,),
        in_specs=[
            pl.BlockSpec((head.shape[0], step), lambda k: (0, k)),
            pl.BlockSpec((n, step), lambda k: (0, k)),
            pl.BlockSpec((n, step), lambda k: (0, k)),
        ],
        out_specs=whole(2 * n, head.shape[0]),
        scratch_shapes=[pltpu.VMEM((2 * n, head.shape[0]), F32)],
        compiler_params=params(1),
        name="project",
    )(head, wm, wo)


def gate_up(at, own, rcv, pick, wm, wo, sm, so):
    n, half = wm.shape[2:]
    weights = pl.BlockSpec((2, 1, n, half), lambda e, c: (0, e, 0, 0))
    return pl.pallas_call(
        gate_up_kernel,
        out_shape=[shape(RING, GATE, 128)] * RING + [shape(RING, UP, 128)] * RING,
        grid_spec=pltpu.PrefetchScalarGridSpec(
            num_scalar_prefetch=1,
            grid=(EXP_DEV,),
            in_specs=[
                whole(*own.shape),
                whole(*rcv.shape),
                pl.BlockSpec((1, CAP, 256), lambda e, c: (e, 0, 0)),
                weights,
                weights,
                whole(*sm.shape),
                whole(*so.shape),
            ],
            out_specs=[whole(RING, GATE, 128)] * RING + [whole(RING, UP, 128)] * RING,
            scratch_shapes=[
                pltpu.VMEM((n, 256), BF),
                pltpu.VMEM((n, 256), BF),
                pltpu.VMEM((2, 256, 256), BF),
                pltpu.VMEM((2, CAP, half), BF),
            ],
        ),
        compiler_params=params(1),
        name="gate_up",
    )(at, own, rcv, pick, wm, wo, sm, so)


def fold(parts):
    return pl.pallas_call(
        fold_kernel,
        out_shape=[shape(*parts[0].shape[1:])] * RING,
        compiler_params=params(),
        name="fold",
    )(*parts)


def activate(gates, ups, pick):
    return pl.pallas_call(
        act_kernel,
        out_shape=shape(CHIPS, ACT, 128),
        compiler_params=params(),
        name="activate",
    )(*gates, *ups, pick)


def down(acts, wm, wo, sm, so, weight, pick):
    n = wm.shape[1]
    return pl.pallas_call(
        down_kernel,
        out_shape=(shape(n, 256, dtype=F32), shape(n, 256)),
        compiler_params=params(),
        name="down",
    )(acts, wm, wo, sm, so, weight, pick)


def halves(value, core, axis):
    size = value.shape[axis] // 2
    mine = lax.dynamic_slice_in_dim(value, core * size, size, axis)
    other = lax.dynamic_slice_in_dim(value, (1 - core) * size, size, axis)
    return mine, other


def by_core(value):
    tail = value.shape[1:]
    return value.reshape(CHIPS, 2, DRAFT, *tail).swapaxes(0, 1).reshape(2 * CHIPS * DRAFT, *tail)


def turned(value):
    return jnp.concatenate([value[2:], value[:2]], 0)


def query_message(q):
    latent = q[:, :LAT].reshape(HALF, 4, 128).swapaxes(0, 1).reshape(4 * HALF, 128)
    rope = q[:, LAT:].reshape(2, HALF // 2, ROPE).swapaxes(0, 1).reshape(HALF // 2, 2 * ROPE)
    return jnp.concatenate([latent, rope], 0)


def per_device(
    queries,
    draft_latents,
    prefix_latents,
    prefix_of,
    accepted,
    w_uv,
    w_out,
    residual,
    norm_gain,
    w_gate_up,
    w_down,
    shared_gate_up,
    shared_down,
    expert_ids,
    expert_gates,
):
    pre = lax.axis_index("pre")
    core, chip = pre % 2, pre // 2
    z, x = chip // RING, chip % RING
    tokens = expert_ids.shape[0]

    q_own = queries[0].swapaxes(0, 1).reshape(ROWS, WIDTH)
    q_first = query_message(q_own[:HALF])
    q_second = query_message(q_own[HALF:])
    first_in = [lax.ppermute(q_first, "pre", X_BY[d]) for d in (1, 3)]
    second_in = [lax.ppermute(q_second, "pre", Z_BY[d]) for d in (1, 3)]
    latents = prefix_latents.swapaxes(1, 2)
    latents_other = swap_core(latents)
    first_in[0], q_first, q_second = lax.optimization_barrier((first_in[0], q_first, q_second))
    first_far = lax.ppermute(q_first, "pre", X_BY[2])
    second_far = lax.ppermute(q_second, "pre", Z_BY[2])
    first = jnp.stack([q_first, first_in[0], first_far, first_in[1]])
    second = jnp.stack([q_second, second_in[0], second_far, second_in[1]])
    first_1, first_3 = [lax.ppermute(first, "pre", Z_BY[d]) for d in (1, 3)]
    second_1, second_3 = [lax.ppermute(second, "pre", X_BY[d]) for d in (1, 3)]
    first_1, first_3, second_1, second_3, w_out = lax.optimization_barrier(
        (first_1, first_3, second_1, second_3, w_out.T)
    )
    w_out_o = swap_core(w_out)
    first_2 = lax.ppermute(turned(first_1), "pre", Z_BY[1])
    second_2 = lax.ppermute(turned(second_1), "pre", X_BY[1])
    sources = (first, first_1, first_3, second, second_1, second_3, first_2, second_2)
    early, late, early_plan, late_plan = [], [], [], []
    for dz, dx in NEAR_SPOTS + FAR_SPOTS:
        spots = tuple(
            (base + {0: 0, 1: 1, 3: 2}[slow], fast) if slow != 2 else (forwarded, (fast + 2) % RING)
            for base, forwarded, slow, fast in ((0, 6, dz, dx), (3, 7, dx, dz))
        )
        if len(early) < SLOTS:
            early.append((dz, dx))
            early_plan.append(spots)
        else:
            late.append((dz, dx))
            late_plan.append(spots)

    def chips_of(spots):
        back = jnp.array(spots, jnp.int32)
        return ((z - back[:, 0]) % RING) * RING + (x - back[:, 1]) % RING

    early_chip, late_chip = chips_of(early), chips_of(late)
    early_out, early_stat = far_first(
        early_plan, jnp.take(prefix_of, early_chip * 2 + core, axis=0), sources[:6], latents, latents_other
    )
    messages = far_second(
        late_plan,
        jnp.take(prefix_of, late_chip * 2 + core, axis=0),
        jnp.concatenate([early_chip, late_chip]),
        sources,
        latents,
        latents_other,
        w_uv,
        early_out,
        early_stat,
    )
    messages, w_out_o, w_gate_up, draft_latents = lax.optimization_barrier(
        (messages, w_out_o, w_gate_up, draft_latents)
    )
    received = chip_exchange(messages)
    pair_m, pair_send = halves(w_gate_up.transpose(2, 0, 1, 3), core, 3)
    near_keys = jnp.pad(draft_latents[0], ((0, 128 - DRAFT), (0, 0)))
    near_out, near_stat = near_part(q_own, near_keys, w_uv)

    received, near_out, pair_send = lax.optimization_barrier((received, near_out, pair_send))
    heads = combine(received, near_out, near_stat)
    held = (residual, norm_gain, w_down, shared_gate_up, shared_down, expert_ids, accepted, pair_send)
    heads, held = lax.optimization_barrier((heads, held))
    residual, norm_gain, w_down, shared_gate_up, shared_down, expert_ids, accepted, pair_send = held
    shared_m, shared_send = halves(shared_gate_up.swapaxes(0, 1), core, 2)
    down_m, down_send = halves(w_down.swapaxes(1, 2), core, 2)
    shared_down_m, shared_down_send = halves(shared_down.T, core, 1)
    token = jnp.arange(tokens, dtype=jnp.int32)
    order = by_core(token)
    to_order = (token[:, None] == order[None, :]).astype(BF)
    skip_m, skip_send = halves(dot(residual.T, to_order).astype(BF), core, 1)
    gain = jnp.broadcast_to(norm_gain[:, None], skip_m.shape)
    misc_m = jnp.concatenate([shared_m, shared_down_m[None], jnp.concatenate([skip_m, gain], 1)[None]], 0)
    misc_send = jnp.concatenate(
        [shared_send, shared_down_send[None], jnp.concatenate([skip_send, gain], 1)[None]], 0
    )
    live = by_core((jnp.arange(DRAFT)[None, :] < accepted[:, None]).reshape(tokens).astype(F32))
    local_experts = lax.axis_index("exp") * EXP_DEV + jnp.arange(EXP_DEV, dtype=jnp.int32)
    chosen = by_core(expert_ids)[:, :, None] == local_experts[None, None, :]
    routed = jnp.any(chosen, 1)
    weights = jnp.sum(jnp.where(chosen, by_core(expert_gates)[:, :, None], 0.0), 1) * live[:, None]
    position = jnp.cumsum(routed.astype(jnp.int32), 0) - 1
    slot_hit = routed.T[:, None, :] & (
        position.T[:, None, :] == jnp.arange(CAP, dtype=jnp.int32)[None, :, None]
    )
    pick = slot_hit.astype(BF)
    slot_weight = jnp.sum(jnp.where(slot_hit, weights.T[:, None, :], 0.0), 2)[:, None, :]
    my_slots = lax.dynamic_slice_in_dim(pick, (chip % 2) * 96, 96, 1).reshape(288, tokens)
    my_tokens = (token[None, :] == (chip % 8) * 32 + jnp.arange(32, dtype=jnp.int32)[:, None]).astype(BF)
    my_pick = jnp.concatenate([my_slots, my_tokens], 0)

    pair_o, down_o, misc_o = [swap_core(v) for v in (pair_send, down_send, misc_send)]
    at = jnp.stack([core, z, x]).astype(jnp.int32)
    head_in = chip_exchange(heads)
    head_in, pair_o, down_o, misc_o, pick, my_pick, slot_weight, at = lax.optimization_barrier(
        (head_in, pair_o, down_o, misc_o, pick, my_pick, slot_weight, at)
    )
    head_out = head_in.reshape(CHIPS * DRAFT, HEADS * HD)
    skip = jnp.concatenate([misc_m[3, :, :128], misc_o[3, :, :128]], 0)
    hidden = skip.astype(F32) + exp_sum(project(head_out, w_out, w_out_o))
    hidden_rcv = swap_core(hidden)

    parts = gate_up(at, hidden, hidden_rcv, pick, pair_m, pair_o, misc_m, misc_o)
    gates, ups = parts[:RING], parts[RING:]
    gates_in = {d: lax.ppermute(gates[d], "pre", X_BY[d]) for d in (2, 1, 3)}
    ups_in = {d: lax.ppermute(ups[d], "pre", Z_BY[d]) for d in (2, 1, 3)}
    gates = fold([gates[0]] + [gates_in[d] for d in (1, 2, 3)])
    ups = fold([ups[0]] + [ups_in[d] for d in (1, 2, 3)])
    gates_in = [lax.ppermute(gates[d], "pre", Z_BY[d]) for d in (1, 3, 2)]
    ups_in = [lax.ppermute(ups[d], "pre", X_BY[d]) for d in (1, 3, 2)]
    acts = activate([gates[0]] + gates_in, [ups[0]] + ups_in, my_pick)
    mine, other = down(
        chip_exchange(acts), down_m, down_o, misc_m, misc_o, slot_weight, pick
    )
    mixed = exp_sum((mine + swap_core(other).astype(F32)).astype(BF))

    n = mine.shape[0]
    kept, other_half = hidden[:n], hidden_rcv[n:]
    hidden_m = jnp.where(
        core == 0, jnp.concatenate([kept, other_half], 1), jnp.concatenate([other_half, kept], 1)
    )
    return dot((hidden_m + mixed).astype(BF), to_order, NT).astype(BF).T


def solution(mesh):
    return jax.shard_map(
        per_device,
        mesh=mesh,
        in_specs=(
            P("pre", None, "exp", None),
            P("pre", None, None),
            P(None, "pre", None),
            P(),
            P(),
            P("exp", None, None),
            P("exp", "pre"),
            P(None, "pre"),
            P("pre"),
            P("exp", "pre", None, None),
            P("exp", None, "pre"),
            P("pre", None, "exp"),
            P("exp", "pre"),
            P(),
            P(),
        ),
        out_specs=P(None, "pre"),
        check_vma=False,
    )
```

```python
import functools
import math

import jax
import jax.numpy as jnp
from jax import lax
from jax.experimental import pallas as pl
from jax.experimental.pallas import tpu as pltpu
from jax.sharding import PartitionSpec as P

D = 7168
LAT = 512
ROPE = 64
HD = 128
DRAFT = 8
EXP_DEV = 3
CAP = 192
RING = 4
CHIPS = 16
HEADS = 32
ROWS = HEADS * DRAFT
MSG = ROWS + 16
HALF = ROWS // 2
WIDTH = LAT + ROPE
QROWS = HALF * WIDTH // 128
GATE = 336
PARTS = (4, 4, 4, 2, 2)
UP = 320
ACT = 320
KEXP = (HD + ROPE) ** (-0.5) * math.log2(math.e)
BF = jnp.bfloat16
F32 = jnp.float32


def device_of(z, x, c):
    return (z * RING + x) * 2 + c


def pre_pairs(move):
    return [
        (device_of(z, x, c), device_of(*move(z, x, c)))
        for z in range(RING)
        for x in range(RING)
        for c in range(2)
    ]


CORE = pre_pairs(lambda z, x, c: (z, x, 1 - c))
X_BY = {d: pre_pairs(lambda z, x, c: (z, (x + d) % RING, c)) for d in (1, 2, 3)}
Z_BY = {d: pre_pairs(lambda z, x, c: ((z + d) % RING, x, c)) for d in (1, 2, 3)}
Y_BY = {d: [(e, (e + d) % RING) for e in range(RING)] for d in (1, 2, 3)}
NEAR_SPOTS = [(0, 0)] + [(dz, dx) for dz in (0, 1, 3) for dx in (0, 1, 3) if dz or dx]
FAR_SPOTS = [(dz, dx) for dz in range(RING) for dx in range(RING) if 2 in (dz, dx)]
SAME_CORE = [[chip * 2 + c for chip in range(CHIPS)] for c in range(2)]


def swap_core(value):
    return lax.ppermute(value, "pre", CORE)


def ring_send(values, pairs):
    return [lax.ppermute(value, "pre", pairs[d]) for d, value in zip((1, 2, 3), values)]


def exp_sum(value):
    others = {d: lax.ppermute(value, "exp", Y_BY[d]).astype(F32) for d in (2, 1, 3)}
    return (value.astype(F32) + others[2]) + (others[1] + others[3])


def chip_exchange(value):
    return lax.all_to_all(value, "pre", 0, 0, axis_index_groups=SAME_CORE)


def dot(a, b, dims=((1,), (0,))):
    return lax.dot_general(a, b, (dims, ((), ())), preferred_element_type=F32)


NT = ((1,), (1,))


def eye(n):
    return lax.broadcasted_iota(jnp.int32, (n, n), 0) == lax.broadcasted_iota(jnp.int32, (n, n), 1)


def column_to_rows(column):
    mask = eye(128)
    parts = [
        jnp.sum(jnp.where(mask, jnp.broadcast_to(column[b * 128 : (b + 1) * 128], (128, 128)), 0.0), 0, keepdims=True)
        for b in range(column.shape[0] // 128)
    ]
    return jnp.concatenate(parts, 0)


def three_terms(rows):
    high = rows.astype(BF).astype(F32)
    rest = rows - high
    mid = rest.astype(BF).astype(F32)
    return [high, mid, rest - mid]


def near_kernel(q_ref, k_ref, w_ref, out_ref, stat_ref, acc):
    keys = k_ref[...]
    scores = dot(q_ref[...], keys, NT)
    draft = lax.broadcasted_iota(jnp.int32, scores.shape, 0) % DRAFT
    key = lax.broadcasted_iota(jnp.int32, scores.shape, 1)
    allowed = key <= draft
    top = jnp.max(jnp.where(allowed, scores, -jnp.inf), 1, keepdims=True)
    weight = jnp.where(allowed, jnp.exp2((scores - top) * KEXP), 0.0).astype(BF)
    total = jnp.sum(weight.astype(F32), 1, keepdims=True)
    acc[...] = dot(weight, keys[:, :LAT])
    stat_ref[...] = jnp.concatenate([column_to_rows(top), column_to_rows(total)], 0)
    for h in range(HEADS):
        rows = slice(h * DRAFT, (h + 1) * DRAFT)
        out_ref[rows, :] = dot(acc[rows, :].astype(BF), w_ref[h])


SLOTS = CHIPS // 2


def attend(q_refs, la_ref, lb_ref, out_ref, stat_ref):
    parts = []
    for b in range(4):
        rows = slice(b * HALF, (b + 1) * HALF)
        parts.append(jnp.concatenate([q[rows, :] for q in q_refs], 0))
    ropes = [q[4 * HALF : QROWS, :] for q in q_refs]
    parts.append(jnp.concatenate([r[:, s : s + ROPE] for r in ropes for s in (0, ROPE)], 0))
    q = jnp.concatenate(parts, 1)
    sa = dot(q, la_ref[...])
    sb = dot(q, lb_ref[...])
    top = jnp.max(jnp.maximum(sa, sb), 1, keepdims=True)
    wa = jnp.exp2((sa - top) * KEXP).astype(BF)
    wb = jnp.exp2((sb - top) * KEXP).astype(BF)
    total = jnp.sum(wa.astype(F32) + wb.astype(F32), 1, keepdims=True)
    out_ref[...] = (dot(wa, la_ref[:LAT], NT) + dot(wb, lb_ref[:LAT], NT)).astype(BF)
    stat_ref[...] = jnp.concatenate(
        [column_to_rows(top), column_to_rows(total), jnp.zeros((4, 128), F32)], 0
    )


def attend_all(plan, prompt, sources, la_ref, lb_ref, out_ref, stat_ref):
    for n, spots in enumerate(plan):
        which = prompt[n]
        q_refs = [sources[source].at[at] for source, at in spots]
        attend(q_refs, la_ref.at[which], lb_ref.at[which], out_ref.at[n], stat_ref.at[n])


def far_first_kernel(plan, prompt, *refs):
    attend_all(plan, prompt, refs[:-4], *refs[-4:])


def far_second_kernel(plan, prompt, place, *refs):
    sources = refs[:-11]
    la_ref, lb_ref, w_ref, early_ref, early_stat, out_ref, acc, stat, early_sem, msg_ref, sems = refs[-11:]
    fetch = pltpu.make_async_copy(early_ref, acc.at[pl.ds(0, SLOTS)], early_sem)
    fetch.start()
    attend_all(plan, prompt, sources, la_ref, lb_ref, acc.at[pl.ds(SLOTS, SLOTS)], stat)
    fetch.wait()
    for n in range(CHIPS):
        rows = early_stat[n] if n < SLOTS else stat[n - SLOTS]
        extra = three_terms(rows[0:2]) + three_terms(rows[2:4]) + [jnp.zeros((4, 128), F32)]
        msg_ref[place[n], ROWS:MSG, :] = jnp.concatenate(extra, 0).astype(BF)
    def send(start, rows, sem):
        part = pl.ds(start, rows)
        return pltpu.make_async_copy(msg_ref.at[:, part, :], out_ref.at[:, part, :], sem)

    send(ROWS, 16, sems.at[HEADS // 4]).start()
    low = lax.broadcasted_iota(jnp.int32, (CHIPS * 16, HD), 0) % 16 < DRAFT

    @pl.loop(0, HEADS // 4)
    def _(quad):
        for r in range(2):
            pair = quad * 2 + r
            start = pl.multiple_of(pair * 16, 16)
            rows = acc[:, pl.ds(start, 16), :].reshape(CHIPS * 16, LAT)
            both = dot(rows, jnp.concatenate([w_ref[pair * 2], w_ref[pair * 2 + 1]], 1))
            picked = jnp.where(low, both[:, :HD], both[:, HD:]).astype(BF)
            for n in range(CHIPS):
                msg_ref[place[n], pl.ds(start, 16), :] = picked[n * 16 : (n + 1) * 16]
        send(pl.multiple_of(quad * 32, 32), 32, sems.at[quad]).start()

    send(ROWS, 16, sems.at[HEADS // 4]).wait()

    @pl.loop(0, HEADS // 4)
    def _(quad):
        send(pl.multiple_of(quad * 32, 32), 32, sems.at[quad]).wait()


def combine_kernel(rec_ref, near_ref, stat_ref, out_ref):
    tops, totals = [], []
    for p in range(CHIPS):
        extra = rec_ref[p, ROWS:MSG, :].astype(F32)
        tops.append(extra[0:2] + extra[2:4] + extra[4:6])
        totals.append(extra[6:8] + extra[8:10] + extra[10:12])
    tops.append(stat_ref[0:2])
    totals.append(stat_ref[2:4])
    best = functools.reduce(jnp.maximum, tops)
    scale = [jnp.exp2((t - best) * KEXP) for t in tops]
    whole = functools.reduce(jnp.add, [s * t for s, t in zip(scale, totals)])
    scale = [s / whole for s in scale]
    blocks = []
    for b in range(2):
        table = jnp.concatenate(
            [s[b : b + 1] for s in scale] + [jnp.zeros((128 - len(scale), 128), F32)], 0
        ).T
        rows = slice(b * 128, (b + 1) * 128)
        value = near_ref[rows, :] * table[:, CHIPS : CHIPS + 1]
        for p in range(CHIPS):
            value = value + rec_ref[p, rows, :].astype(F32) * table[:, p : p + 1]
        blocks.append(value)
    value = jnp.concatenate(blocks, 0)
    flat = jnp.concatenate([value[h * DRAFT : (h + 1) * DRAFT] for h in range(HEADS)], 1).astype(BF)
    for p in range(CHIPS):
        out_ref[p] = flat


CUTS = 4


def project_kernel(head_ref, wm_ref, wo_ref, out_ref, head, weight, sems):
    step = head.shape[1] // CUTS
    copies = []
    for c in range(CUTS):
        part = pl.ds(c * step, step)
        copies.append(
            [
                pltpu.make_async_copy(head_ref.at[:, part], head.at[:, part], sems.at[c, 0]),
                pltpu.make_async_copy(wm_ref.at[:, part], weight.at[0, :, part], sems.at[c, 1]),
                pltpu.make_async_copy(wo_ref.at[:, part], weight.at[1, :, part], sems.at[c, 2]),
            ]
        )
    for group in copies:
        for copy in group:
            copy.start()
    totals = [0.0, 0.0]
    for c, group in enumerate(copies):
        for copy in group:
            copy.wait()
        part = slice(c * step, (c + 1) * step)
        totals = [t + dot(weight[k, :, part], head[:, part], NT) for k, t in enumerate(totals)]
    out_ref[...] = jnp.concatenate(totals, 0).astype(BF)


def gate_up_kernel(
    at_ref, own_ref, rcv_ref, pick_ref, wm_ref, wo_ref, sm_ref, so_ref, *refs
):
    outs, (xm, xo, pair, wide) = refs[:10], refs[10:]
    e = pl.program_id(0)
    core, z, x = at_ref[0], at_ref[1], at_ref[2]
    n = xm.shape[0]

    def spot(group, slow, fast):
        if slow == 2:
            return group[3 + fast // 2].at[fast % 2]
        return group[{0: 0, 1: 1, 3: 2}[slow]].at[fast]

    def destinations():
        for dx in range(RING):
            for dz in range(RING):
                chip = lax.rem(z + dz, RING) * RING + lax.rem(x + dx, RING)
                yield (spot(outs[:5], dx, dz), spot(outs[5:], dz, dx)), chip

    @pl.when(e == 0)
    def _():
        square = jnp.zeros((1, 256), F32)
        for keep, misc_ref, mine, theirs in ((xm, sm_ref, 0, n), (xo, so_ref, n, 0)):
            own = own_ref[mine : mine + n, :]
            rcv = rcv_ref[theirs : theirs + n, :]
            whole = jnp.concatenate([jnp.where(core == 0, own, rcv), jnp.where(core == 0, rcv, own)], 1)
            square = square + jnp.sum(whole * whole, 0, keepdims=True)
            keep[...] = (whole * misc_ref[3][:, 128:129].astype(F32)).astype(BF)
        terms = three_terms(jnp.concatenate([square[:, :128], square[:, 128:]], 0))
        rows = jnp.concatenate(terms + [jnp.zeros((10, 128), F32)], 0).astype(BF)
        same = eye(256).astype(BF)
        all_m = dot(same, xm[...], NT).astype(BF)
        all_o = dot(same, xo[...], NT).astype(BF)
        for g in range(2):
            pair[g] = (dot(all_m, sm_ref[g]) + dot(all_o, so_ref[g])).astype(BF)
        for pieces, chip in destinations():
            pieces[0][320:336, :] = rows
            top = pl.multiple_of(lax.rem(chip, 8) * 32, 32)
            left = pl.multiple_of(lax.div(chip, 8) * 128, 128)
            for g in range(2):
                pieces[g][288:320, :] = pair[g, pl.ds(top, 32), pl.ds(left, 128)]

    picked_m = dot(pick_ref[0], xm[...], NT).astype(BF)
    picked_o = dot(pick_ref[0], xo[...], NT).astype(BF)
    for g in range(2):
        wide[g] = (dot(picked_m, wm_ref[g, 0]) + dot(picked_o, wo_ref[g, 0])).astype(BF)
    start = pl.multiple_of(e * 96, 32)
    for pieces, chip in destinations():
        top = pl.multiple_of(lax.rem(chip, 2) * 96, 32)
        left = pl.multiple_of(lax.div(chip, 2) * 128, 128)
        for g in range(2):
            pieces[g][pl.ds(start, 96), :] = wide[g, pl.ds(top, 96), pl.ds(left, 128)]


def pass_on_kernel(one, three, from_back, from_ahead, one_out, three_out):
    one_out[:2] = (one[:2].astype(F32) + from_back[...].astype(F32)).astype(BF)
    one_out[2:] = one[2:]
    three_out[:2] = three[:2]
    three_out[2:] = (three[2:].astype(F32) + from_ahead[...].astype(F32)).astype(BF)


def fold_kernel(*refs):
    ins, outs = refs[:-RING], refs[-RING:]
    for k in range(RING):
        total = ins[0][k].astype(F32)
        for r in ins[1:]:
            total = total + r[k].astype(F32)
        outs[k][...] = total.astype(BF)


def act_kernel(*refs):
    gates, ups, pick_ref, out_ref = refs[:RING], refs[RING : 2 * RING], refs[-2], refs[-1]

    def total(parts):
        return functools.reduce(jnp.add, [part[...].astype(F32) for part in parts])

    gate, up = total(gates), total(ups)
    square = gate[320:322] + gate[322:324] + gate[324:326]
    inverse = lax.rsqrt(square / D + 1e-06)
    pick = pick_ref[...].astype(F32)
    factor = jnp.sum(pick[:, :128] * inverse[0:1] + pick[:, 128:] * inverse[1:2], 1, keepdims=True)
    act = (jax.nn.silu(gate[:ACT] * factor) * (up * factor)).astype(BF)
    for p in range(CHIPS):
        out_ref[p] = act


def down_kernel(act_ref, wm_ref, wo_ref, sm_ref, so_ref, weight_ref, pick_ref, mine_ref, other_ref):
    pieces = []
    for e in range(EXP_DEV):
        rows = slice(e * 96, (e + 1) * 96)
        pieces.append(
            jnp.concatenate(
                [jnp.concatenate([act_ref[u * 2 + half, rows, :] for u in range(8)], 1) for half in range(2)], 0
            )
        )
    shared = jnp.concatenate(
        [jnp.concatenate([act_ref[u * 8 + t, 288:320, :] for u in range(2)], 1) for t in range(8)], 0
    )
    for w_ref, s_ref, out_ref in ((wm_ref, sm_ref, mine_ref), (wo_ref, so_ref, other_ref)):
        total = dot(s_ref[2], shared, NT)
        for e in range(EXP_DEV):
            weighted = (dot(w_ref[e], pieces[e], NT) * weight_ref[e]).astype(BF)
            total = total + dot(weighted, pick_ref[e])
        out_ref[...] = total.astype(out_ref.dtype)


def params(n=0, limit=24):
    size = limit * 1024 * 1024
    if n:
        return pltpu.CompilerParams(vmem_limit_bytes=size, dimension_semantics=("arbitrary",) * n)
    return pltpu.CompilerParams(vmem_limit_bytes=size)


def shape(*dims, dtype=BF):
    return jax.ShapeDtypeStruct(dims, dtype)


def whole(*dims):
    return pl.BlockSpec(dims, lambda *at: (0,) * len(dims))


def near_part(q, keys, w_uv):
    return pl.pallas_call(
        near_kernel,
        out_shape=(shape(ROWS, HD, dtype=F32), shape(4, 128, dtype=F32)),
        scratch_shapes=[pltpu.VMEM((ROWS, LAT), F32)],
        compiler_params=params(),
        name="near",
    )(q, keys, w_uv)


def vmem():
    return pl.BlockSpec(memory_space=pltpu.VMEM)


def far_cost():
    rows = SLOTS * ROWS
    return pl.CostEstimate(
        flops=2 * rows * 1024 * (WIDTH + LAT), bytes_accessed=24 * 1024 * 1024, transcendentals=rows * 1024
    )


def far_first(plan, prompt, sources, la, lb):
    return pl.pallas_call(
        functools.partial(far_first_kernel, plan),
        out_shape=(shape(SLOTS, ROWS, LAT), shape(SLOTS, 8, 128, dtype=F32)),
        in_specs=[pl.BlockSpec(memory_space=pltpu.SMEM)]
        + [vmem()] * len(sources)
        + [vmem(), vmem()],
        out_specs=(vmem(), vmem()),
        compiler_params=params(limit=18),
        cost_estimate=far_cost(),
        name="far_first",
    )(prompt, *sources, la, lb)


def far_second(plan, prompt, place, sources, la, lb, w_uv, early, early_stat):
    return pl.pallas_call(
        functools.partial(far_second_kernel, plan),
        out_shape=shape(CHIPS, MSG, HD),
        in_specs=[pl.BlockSpec(memory_space=pltpu.SMEM)] * 2
        + [vmem()] * len(sources)
        + [vmem(), vmem(), vmem(), pl.BlockSpec(memory_space=pl.ANY), vmem()],
        out_specs=pl.BlockSpec(memory_space=pltpu.HBM),
        scratch_shapes=[
            pltpu.VMEM((CHIPS, ROWS, LAT), BF),
            pltpu.VMEM((SLOTS, 8, 128), F32),
            pltpu.SemaphoreType.DMA,
            pltpu.VMEM((CHIPS, MSG, HD), BF),
            pltpu.SemaphoreType.DMA((HEADS // 4 + 1,)),
        ],
        compiler_params=params(limit=24),
        cost_estimate=far_cost(),
        name="far_second",
    )(prompt, place, *sources, la, lb, w_uv, early, early_stat)


def combine(received, near_out, near_stat):
    return pl.pallas_call(
        combine_kernel,
        out_shape=shape(CHIPS, DRAFT, HEADS * HD),
        compiler_params=params(),
        name="combine",
    )(received, near_out, near_stat)


def project(head, wm, wo):
    n, depth = wm.shape
    return pl.pallas_call(
        project_kernel,
        out_shape=shape(2 * n, head.shape[0]),
        in_specs=[pl.BlockSpec(memory_space=pltpu.HBM)] * 3,
        scratch_shapes=[
            pltpu.VMEM(head.shape, BF),
            pltpu.VMEM((2, n, depth), BF),
            pltpu.SemaphoreType.DMA((CUTS, 3)),
        ],
        compiler_params=params(),
        name="project",
    )(head, wm, wo)


def gate_up(at, own, rcv, pick, wm, wo, sm, so):
    n, half = wm.shape[2:]
    weights = pl.BlockSpec((2, 1, n, half), lambda e, c: (0, e, 0, 0))
    return pl.pallas_call(
        gate_up_kernel,
        out_shape=[shape(n, rows, 128) for rows in (GATE, UP) for n in PARTS],
        grid_spec=pltpu.PrefetchScalarGridSpec(
            num_scalar_prefetch=1,
            grid=(EXP_DEV,),
            in_specs=[
                whole(*own.shape),
                whole(*rcv.shape),
                pl.BlockSpec((1, CAP, 256), lambda e, c: (e, 0, 0)),
                weights,
                weights,
                whole(*sm.shape),
                whole(*so.shape),
            ],
            out_specs=[whole(n, rows, 128) for rows in (GATE, UP) for n in PARTS],
            scratch_shapes=[
                pltpu.VMEM((n, 256), BF),
                pltpu.VMEM((n, 256), BF),
                pltpu.VMEM((2, 256, 256), BF),
                pltpu.VMEM((2, CAP, half), BF),
            ],
        ),
        compiler_params=params(1),
        name="gate_up",
    )(at, own, rcv, pick, wm, wo, sm, so)


def pass_on(one, three, from_back, from_ahead):
    return pl.pallas_call(
        pass_on_kernel,
        out_shape=[shape(*one.shape)] * 2,
        compiler_params=params(),
        name="pass_on",
    )(one, three, from_back, from_ahead)


def fold(parts):
    return pl.pallas_call(
        fold_kernel,
        out_shape=[shape(*parts[0].shape[1:])] * RING,
        compiler_params=params(),
        name="fold",
    )(*parts)


def activate(gates, ups, pick):
    return pl.pallas_call(
        act_kernel,
        out_shape=shape(CHIPS, ACT, 128),
        compiler_params=params(),
        name="activate",
    )(*gates, *ups, pick)


def down(acts, wm, wo, sm, so, weight, pick):
    n = wm.shape[1]
    return pl.pallas_call(
        down_kernel,
        out_shape=(shape(n, 256, dtype=F32), shape(n, 256)),
        compiler_params=params(),
        name="down",
    )(acts, wm, wo, sm, so, weight, pick)


def halves(value, core, axis):
    size = value.shape[axis] // 2
    mine = lax.dynamic_slice_in_dim(value, core * size, size, axis)
    other = lax.dynamic_slice_in_dim(value, (1 - core) * size, size, axis)
    return mine, other


def by_core(value):
    tail = value.shape[1:]
    return value.reshape(CHIPS, 2, DRAFT, *tail).swapaxes(0, 1).reshape(2 * CHIPS * DRAFT, *tail)


def turned(value):
    return jnp.concatenate([value[2:], value[:2]], 0)


def query_message(q):
    latent = q[:, :LAT].reshape(HALF, 4, 128).swapaxes(0, 1).reshape(4 * HALF, 128)
    rope = q[:, LAT:].reshape(2, HALF // 2, ROPE).swapaxes(0, 1).reshape(HALF // 2, 2 * ROPE)
    return jnp.concatenate([latent, rope], 0)


def per_device(
    queries,
    draft_latents,
    prefix_latents,
    prefix_of,
    accepted,
    w_uv,
    w_out,
    residual,
    norm_gain,
    w_gate_up,
    w_down,
    shared_gate_up,
    shared_down,
    expert_ids,
    expert_gates,
):
    pre = lax.axis_index("pre")
    core, chip = pre % 2, pre // 2
    z, x = chip // RING, chip % RING
    tokens = expert_ids.shape[0]

    q_own = queries[0].swapaxes(0, 1).reshape(ROWS, WIDTH)
    q_first = query_message(q_own[:HALF])
    q_second = query_message(q_own[HALF:])
    first_in = [lax.ppermute(q_first, "pre", X_BY[d]) for d in (1, 3)]
    second_in = [lax.ppermute(q_second, "pre", Z_BY[d]) for d in (1, 3)]
    latents = prefix_latents.swapaxes(1, 2)
    latents_other = swap_core(latents)
    first_in[0], q_first, q_second = lax.optimization_barrier((first_in[0], q_first, q_second))
    first_far = lax.ppermute(q_first, "pre", X_BY[2])
    second_far = lax.ppermute(q_second, "pre", Z_BY[2])
    first = jnp.stack([q_first, first_in[0], first_far, first_in[1]])
    second = jnp.stack([q_second, second_in[0], second_far, second_in[1]])
    first_1, first_3 = [lax.ppermute(first, "pre", Z_BY[d]) for d in (1, 3)]
    second_1, second_3 = [lax.ppermute(second, "pre", X_BY[d]) for d in (1, 3)]
    first_1, first_3, second_1, second_3, w_out = lax.optimization_barrier(
        (first_1, first_3, second_1, second_3, w_out.T)
    )
    w_out_o = swap_core(w_out)
    first_2 = lax.ppermute(turned(first_1), "pre", Z_BY[1])
    second_2 = lax.ppermute(turned(second_1), "pre", X_BY[1])
    sources = (first, first_1, first_3, second, second_1, second_3, first_2, second_2)
    early, late, early_plan, late_plan = [], [], [], []
    for dz, dx in NEAR_SPOTS + FAR_SPOTS:
        spots = tuple(
            (base + {0: 0, 1: 1, 3: 2}[slow], fast) if slow != 2 else (forwarded, (fast + 2) % RING)
            for base, forwarded, slow, fast in ((0, 6, dz, dx), (3, 7, dx, dz))
        )
        if len(early) < SLOTS:
            early.append((dz, dx))
            early_plan.append(spots)
        else:
            late.append((dz, dx))
            late_plan.append(spots)

    def chips_of(spots):
        back = jnp.array(spots, jnp.int32)
        return ((z - back[:, 0]) % RING) * RING + (x - back[:, 1]) % RING

    early_chip, late_chip = chips_of(early), chips_of(late)
    early_out, early_stat = far_first(
        early_plan, jnp.take(prefix_of, early_chip * 2 + core, axis=0), sources[:6], latents, latents_other
    )
    messages = far_second(
        late_plan,
        jnp.take(prefix_of, late_chip * 2 + core, axis=0),
        jnp.concatenate([early_chip, late_chip]),
        sources,
        latents,
        latents_other,
        w_uv,
        early_out,
        early_stat,
    )
    messages, w_gate_up, draft_latents = lax.optimization_barrier((messages, w_gate_up, draft_latents))
    received = chip_exchange(messages)
    pair_m, pair_send = halves(w_gate_up.transpose(2, 0, 1, 3), core, 3)
    near_keys = jnp.pad(draft_latents[0], ((0, 128 - DRAFT), (0, 0)))
    near_out, near_stat = near_part(q_own, near_keys, w_uv)

    received, near_out, pair_send = lax.optimization_barrier((received, near_out, pair_send))
    heads = combine(received, near_out, near_stat)
    held = (residual, norm_gain, w_down, shared_gate_up, shared_down, expert_ids, accepted, pair_send)
    heads, held = lax.optimization_barrier((heads, held))
    residual, norm_gain, w_down, shared_gate_up, shared_down, expert_ids, accepted, pair_send = held
    shared_m, shared_send = halves(shared_gate_up.swapaxes(0, 1), core, 2)
    down_m, down_send = halves(w_down.swapaxes(1, 2), core, 2)
    shared_down_m, shared_down_send = halves(shared_down.T, core, 1)
    token = jnp.arange(tokens, dtype=jnp.int32)
    order = by_core(token)
    to_order = (token[:, None] == order[None, :]).astype(BF)
    skip_m, skip_send = halves(dot(residual.T, to_order).astype(BF), core, 1)
    gain = jnp.broadcast_to(norm_gain[:, None], skip_m.shape)
    misc_m = jnp.concatenate([shared_m, shared_down_m[None], jnp.concatenate([skip_m, gain], 1)[None]], 0)
    misc_send = jnp.concatenate(
        [shared_send, shared_down_send[None], jnp.concatenate([skip_send, gain], 1)[None]], 0
    )
    live = by_core((jnp.arange(DRAFT)[None, :] < accepted[:, None]).reshape(tokens).astype(F32))
    local_experts = lax.axis_index("exp") * EXP_DEV + jnp.arange(EXP_DEV, dtype=jnp.int32)
    chosen = by_core(expert_ids)[:, :, None] == local_experts[None, None, :]
    routed = jnp.any(chosen, 1)
    weights = jnp.sum(jnp.where(chosen, by_core(expert_gates)[:, :, None], 0.0), 1) * live[:, None]
    position = jnp.cumsum(routed.astype(jnp.int32), 0) - 1
    slot_hit = routed.T[:, None, :] & (
        position.T[:, None, :] == jnp.arange(CAP, dtype=jnp.int32)[None, :, None]
    )
    pick = slot_hit.astype(BF)
    slot_weight = jnp.sum(jnp.where(slot_hit, weights.T[:, None, :], 0.0), 2)[:, None, :]
    my_slots = lax.dynamic_slice_in_dim(pick, (chip % 2) * 96, 96, 1).reshape(288, tokens)
    my_tokens = (token[None, :] == (chip % 8) * 32 + jnp.arange(32, dtype=jnp.int32)[:, None]).astype(BF)
    my_pick = jnp.concatenate([my_slots, my_tokens], 0)

    pair_o, down_o, misc_o = [swap_core(v) for v in (pair_send, down_send, misc_send)]
    at = jnp.stack([core, z, x]).astype(jnp.int32)
    head_in = chip_exchange(heads)
    head_in, pair_o, down_o, misc_o, misc_m, pick, my_pick, slot_weight, at = lax.optimization_barrier(
        (head_in, pair_o, down_o, misc_o, misc_m, pick, my_pick, slot_weight, at)
    )
    head_out = head_in.reshape(CHIPS * DRAFT, HEADS * HD)
    skip = jnp.concatenate([misc_m[3, :, :128], misc_o[3, :, :128]], 0)
    hidden = skip.astype(F32) + exp_sum(project(head_out, w_out, w_out_o))
    hidden_rcv = swap_core(hidden)

    parts = gate_up(at, hidden, hidden_rcv, pick, pair_m, pair_o, misc_m, misc_o)
    gates, ups = parts[:5], parts[5:]
    gates_in = [lax.ppermute(gates[3], "pre", X_BY[1]), lax.ppermute(gates[4], "pre", X_BY[3])]
    ups_in = [lax.ppermute(ups[3], "pre", Z_BY[1]), lax.ppermute(ups[4], "pre", Z_BY[3])]
    gates_on = pass_on(gates[1], gates[2], *gates_in)
    ups_on = pass_on(ups[1], ups[2], *ups_in)
    gates_in = [lax.ppermute(gates_on[0], "pre", X_BY[1]), lax.ppermute(gates_on[1], "pre", X_BY[3])]
    ups_in = [lax.ppermute(ups_on[0], "pre", Z_BY[1]), lax.ppermute(ups_on[1], "pre", Z_BY[3])]
    gates = fold([gates[0]] + gates_in)
    ups = fold([ups[0]] + ups_in)
    gates_in = [lax.ppermute(gates[d], "pre", Z_BY[d]) for d in (1, 3, 2)]
    ups_in = [lax.ppermute(ups[d], "pre", X_BY[d]) for d in (1, 3, 2)]
    acts = activate([gates[0]] + gates_in, [ups[0]] + ups_in, my_pick)
    mine, other = down(
        chip_exchange(acts), down_m, down_o, misc_m, misc_o, slot_weight, pick
    )
    mixed = exp_sum((mine + swap_core(other).astype(F32)).astype(BF))

    n = mine.shape[0]
    kept, other_half = hidden[:n], hidden_rcv[n:]
    hidden_m = jnp.where(
        core == 0, jnp.concatenate([kept, other_half], 1), jnp.concatenate([other_half, kept], 1)
    )
    return dot((hidden_m + mixed).astype(BF), to_order, NT).astype(BF).T


def solution(mesh):
    return jax.shard_map(
        per_device,
        mesh=mesh,
        in_specs=(
            P("pre", None, "exp", None),
            P("pre", None, None),
            P(None, "pre", None),
            P(),
            P(),
            P("exp", None, None),
            P("exp", "pre"),
            P(None, "pre"),
            P("pre"),
            P("exp", "pre", None, None),
            P("exp", None, "pre"),
            P("pre", None, "exp"),
            P("exp", "pre"),
            P(),
            P(),
        ),
        out_specs=P(None, "pre"),
        check_vma=False,
    )
```

```python
import functools
import math

import jax
import jax.numpy as jnp
from jax import lax
from jax.experimental import pallas as pl
from jax.experimental.pallas import tpu as pltpu
from jax.sharding import PartitionSpec as P

D = 7168
LAT = 512
ROPE = 64
HD = 128
DRAFT = 8
EXP_DEV = 3
CAP = 192
RING = 4
CHIPS = 16
HEADS = 32
ROWS = HEADS * DRAFT
MSG = ROWS + 16
HALF = ROWS // 2
WIDTH = LAT + ROPE
QROWS = HALF * WIDTH // 128
GATE = 336
PARTS = (4, 4, 4, 2, 2)
UP = 320
ACT = 320
KEXP = (HD + ROPE) ** (-0.5) * math.log2(math.e)
BF = jnp.bfloat16
F32 = jnp.float32


def device_of(z, x, c):
    return (z * RING + x) * 2 + c


def pre_pairs(move):
    return [
        (device_of(z, x, c), device_of(*move(z, x, c)))
        for z in range(RING)
        for x in range(RING)
        for c in range(2)
    ]


CORE = pre_pairs(lambda z, x, c: (z, x, 1 - c))
X_BY = {d: pre_pairs(lambda z, x, c: (z, (x + d) % RING, c)) for d in (1, 2, 3)}
Z_BY = {d: pre_pairs(lambda z, x, c: ((z + d) % RING, x, c)) for d in (1, 2, 3)}
Y_BY = {d: [(e, (e + d) % RING) for e in range(RING)] for d in (1, 2, 3)}
NEAR_SPOTS = [(0, 0)] + [(dz, dx) for dz in (0, 1, 3) for dx in (0, 1, 3) if dz or dx]
FAR_SPOTS = [(dz, dx) for dz in range(RING) for dx in range(RING) if 2 in (dz, dx)]
SAME_CORE = [[chip * 2 + c for chip in range(CHIPS)] for c in range(2)]


def swap_core(value):
    return lax.ppermute(value, "pre", CORE)


def ring_send(values, pairs):
    return [lax.ppermute(value, "pre", pairs[d]) for d, value in zip((1, 2, 3), values)]


def exp_sum(value):
    others = {d: lax.ppermute(value, "exp", Y_BY[d]).astype(F32) for d in (2, 1, 3)}
    return (value.astype(F32) + others[2]) + (others[1] + others[3])


def chip_exchange(value):
    return lax.all_to_all(value, "pre", 0, 0, axis_index_groups=SAME_CORE)


def dot(a, b, dims=((1,), (0,))):
    return lax.dot_general(a, b, (dims, ((), ())), preferred_element_type=F32)


NT = ((1,), (1,))


def eye(n):
    return lax.broadcasted_iota(jnp.int32, (n, n), 0) == lax.broadcasted_iota(jnp.int32, (n, n), 1)


def column_to_rows(column):
    mask = eye(128)
    parts = [
        jnp.sum(jnp.where(mask, jnp.broadcast_to(column[b * 128 : (b + 1) * 128], (128, 128)), 0.0), 0, keepdims=True)
        for b in range(column.shape[0] // 128)
    ]
    return jnp.concatenate(parts, 0)


def three_terms(rows):
    high = rows.astype(BF).astype(F32)
    rest = rows - high
    mid = rest.astype(BF).astype(F32)
    return [high, mid, rest - mid]


def near_kernel(q_ref, k_ref, w_ref, out_ref, stat_ref, acc):
    keys = k_ref[...]
    scores = dot(q_ref[...], keys, NT)
    draft = lax.broadcasted_iota(jnp.int32, scores.shape, 0) % DRAFT
    key = lax.broadcasted_iota(jnp.int32, scores.shape, 1)
    allowed = key <= draft
    top = jnp.max(jnp.where(allowed, scores, -jnp.inf), 1, keepdims=True)
    weight = jnp.where(allowed, jnp.exp2((scores - top) * KEXP), 0.0).astype(BF)
    total = jnp.sum(weight.astype(F32), 1, keepdims=True)
    acc[...] = dot(weight, keys[:, :LAT])
    stat_ref[...] = jnp.concatenate([column_to_rows(top), column_to_rows(total)], 0)
    for h in range(HEADS):
        rows = slice(h * DRAFT, (h + 1) * DRAFT)
        out_ref[rows, :] = dot(acc[rows, :].astype(BF), w_ref[h])


SLOTS = CHIPS // 2


def attend(q_refs, la_ref, lb_ref, out_ref, stat_ref):
    parts = []
    for b in range(4):
        rows = slice(b * HALF, (b + 1) * HALF)
        parts.append(jnp.concatenate([q[rows, :] for q in q_refs], 0))
    ropes = [q[4 * HALF : QROWS, :] for q in q_refs]
    parts.append(jnp.concatenate([r[:, s : s + ROPE] for r in ropes for s in (0, ROPE)], 0))
    q = jnp.concatenate(parts, 1)
    sa = dot(q, la_ref[...])
    sb = dot(q, lb_ref[...])
    top = jnp.max(jnp.maximum(sa, sb), 1, keepdims=True)
    wa = jnp.exp2((sa - top) * KEXP).astype(BF)
    wb = jnp.exp2((sb - top) * KEXP).astype(BF)
    total = jnp.sum(wa.astype(F32) + wb.astype(F32), 1, keepdims=True)
    out_ref[...] = (dot(wa, la_ref[:LAT], NT) + dot(wb, lb_ref[:LAT], NT)).astype(BF)
    stat_ref[...] = jnp.concatenate(
        [column_to_rows(top), column_to_rows(total), jnp.zeros((4, 128), F32)], 0
    )


def attend_all(plan, prompt, sources, la_ref, lb_ref, out_ref, stat_ref):
    for n, spots in enumerate(plan):
        which = prompt[n]
        q_refs = [sources[source].at[at] for source, at in spots]
        attend(q_refs, la_ref.at[which], lb_ref.at[which], out_ref.at[n], stat_ref.at[n])


def far_first_kernel(plan, prompt, *refs):
    attend_all(plan, prompt, refs[:-4], *refs[-4:])


def far_second_kernel(plan, prompt, place, *refs):
    sources = refs[:-11]
    la_ref, lb_ref, w_ref, early_ref, early_stat, out_ref, acc, stat, early_sem, msg_ref, sems = refs[-11:]
    fetch = pltpu.make_async_copy(early_ref, acc.at[pl.ds(0, SLOTS)], early_sem)
    fetch.start()
    attend_all(plan, prompt, sources, la_ref, lb_ref, acc.at[pl.ds(SLOTS, SLOTS)], stat)
    fetch.wait()
    for n in range(CHIPS):
        rows = early_stat[n] if n < SLOTS else stat[n - SLOTS]
        extra = three_terms(rows[0:2]) + three_terms(rows[2:4]) + [jnp.zeros((4, 128), F32)]
        msg_ref[place[n], ROWS:MSG, :] = jnp.concatenate(extra, 0).astype(BF)
    def send(start, rows, sem):
        part = pl.ds(start, rows)
        return pltpu.make_async_copy(msg_ref.at[:, part, :], out_ref.at[:, part, :], sem)

    send(ROWS, 16, sems.at[HEADS // 4]).start()
    low = lax.broadcasted_iota(jnp.int32, (CHIPS * 16, HD), 0) % 16 < DRAFT

    @pl.loop(0, HEADS // 4)
    def _(quad):
        for r in range(2):
            pair = quad * 2 + r
            start = pl.multiple_of(pair * 16, 16)
            rows = acc[:, pl.ds(start, 16), :].reshape(CHIPS * 16, LAT)
            both = dot(rows, jnp.concatenate([w_ref[pair * 2], w_ref[pair * 2 + 1]], 1))
            picked = jnp.where(low, both[:, :HD], both[:, HD:]).astype(BF)
            for n in range(CHIPS):
                msg_ref[place[n], pl.ds(start, 16), :] = picked[n * 16 : (n + 1) * 16]
        send(pl.multiple_of(quad * 32, 32), 32, sems.at[quad]).start()

    send(ROWS, 16, sems.at[HEADS // 4]).wait()

    @pl.loop(0, HEADS // 4)
    def _(quad):
        send(pl.multiple_of(quad * 32, 32), 32, sems.at[quad]).wait()


def combine_kernel(rec_ref, near_ref, stat_ref, out_ref):
    tops, totals = [], []
    for p in range(CHIPS):
        extra = rec_ref[p, ROWS:MSG, :].astype(F32)
        tops.append(extra[0:2] + extra[2:4] + extra[4:6])
        totals.append(extra[6:8] + extra[8:10] + extra[10:12])
    tops.append(stat_ref[0:2])
    totals.append(stat_ref[2:4])
    best = functools.reduce(jnp.maximum, tops)
    scale = [jnp.exp2((t - best) * KEXP) for t in tops]
    whole = functools.reduce(jnp.add, [s * t for s, t in zip(scale, totals)])
    scale = [s / whole for s in scale]
    blocks = []
    for b in range(2):
        table = jnp.concatenate(
            [s[b : b + 1] for s in scale] + [jnp.zeros((128 - len(scale), 128), F32)], 0
        ).T
        rows = slice(b * 128, (b + 1) * 128)
        value = near_ref[rows, :] * table[:, CHIPS : CHIPS + 1]
        for p in range(CHIPS):
            value = value + rec_ref[p, rows, :].astype(F32) * table[:, p : p + 1]
        blocks.append(value)
    value = jnp.concatenate(blocks, 0)
    flat = jnp.concatenate([value[h * DRAFT : (h + 1) * DRAFT] for h in range(HEADS)], 1).astype(BF)
    for p in range(CHIPS):
        out_ref[p] = flat


CUTS = 4


def project_kernel(head_ref, wm_ref, wo_ref, out_ref, head, weight, sems):
    step = head.shape[1] // CUTS
    copies = []
    for c in range(CUTS):
        part = pl.ds(c * step, step)
        copies.append(
            [
                pltpu.make_async_copy(head_ref.at[:, part], head.at[:, part], sems.at[c, 0]),
                pltpu.make_async_copy(wm_ref.at[:, part], weight.at[0, :, part], sems.at[c, 1]),
                pltpu.make_async_copy(wo_ref.at[:, part], weight.at[1, :, part], sems.at[c, 2]),
            ]
        )
    for group in copies:
        for copy in group:
            copy.start()
    totals = [0.0, 0.0]
    for c, group in enumerate(copies):
        for copy in group:
            copy.wait()
        part = slice(c * step, (c + 1) * step)
        totals = [t + dot(weight[k, :, part], head[:, part], NT) for k, t in enumerate(totals)]
    out_ref[...] = jnp.concatenate(totals, 0).astype(BF)


def gate_up_kernel(
    at_ref, own_ref, rcv_ref, pick_ref, wm_ref, wo_ref, sm_ref, so_ref, *refs
):
    outs, (xm, xo, pair, wide) = refs[:10], refs[10:]
    e = pl.program_id(0)
    core, z, x = at_ref[0], at_ref[1], at_ref[2]
    n = xm.shape[0]

    def spot(group, slow, fast):
        if slow == 2:
            return group[3 + fast // 2].at[fast % 2]
        return group[{0: 0, 1: 1, 3: 2}[slow]].at[fast]

    def destinations():
        for dx in range(RING):
            for dz in range(RING):
                chip = lax.rem(z + dz, RING) * RING + lax.rem(x + dx, RING)
                yield (spot(outs[:5], dx, dz), spot(outs[5:], dz, dx)), chip

    @pl.when(e == 0)
    def _():
        square = jnp.zeros((1, 256), F32)
        for keep, misc_ref, mine, theirs in ((xm, sm_ref, 0, n), (xo, so_ref, n, 0)):
            own = own_ref[mine : mine + n, :]
            rcv = rcv_ref[theirs : theirs + n, :]
            whole = jnp.concatenate([jnp.where(core == 0, own, rcv), jnp.where(core == 0, rcv, own)], 1)
            square = square + jnp.sum(whole * whole, 0, keepdims=True)
            keep[...] = (whole * misc_ref[3][:, 128:129].astype(F32)).astype(BF)
        terms = three_terms(jnp.concatenate([square[:, :128], square[:, 128:]], 0))
        rows = jnp.concatenate(terms + [jnp.zeros((10, 128), F32)], 0).astype(BF)
        same = eye(256).astype(BF)
        all_m = dot(same, xm[...], NT).astype(BF)
        all_o = dot(same, xo[...], NT).astype(BF)
        for g in range(2):
            pair[g] = (dot(all_m, sm_ref[g]) + dot(all_o, so_ref[g])).astype(BF)
        for pieces, chip in destinations():
            pieces[0][320:336, :] = rows
            top = pl.multiple_of(lax.rem(chip, 8) * 32, 32)
            left = pl.multiple_of(lax.div(chip, 8) * 128, 128)
            for g in range(2):
                pieces[g][288:320, :] = pair[g, pl.ds(top, 32), pl.ds(left, 128)]

    picked_m = dot(pick_ref[0], xm[...], NT).astype(BF)
    picked_o = dot(pick_ref[0], xo[...], NT).astype(BF)
    for g in range(2):
        wide[g] = (dot(picked_m, wm_ref[g, 0]) + dot(picked_o, wo_ref[g, 0])).astype(BF)
    start = pl.multiple_of(e * 96, 32)
    for pieces, chip in destinations():
        top = pl.multiple_of(lax.rem(chip, 2) * 96, 32)
        left = pl.multiple_of(lax.div(chip, 2) * 128, 128)
        for g in range(2):
            pieces[g][pl.ds(start, 96), :] = wide[g, pl.ds(top, 96), pl.ds(left, 128)]


def pass_on_kernel(one, three, from_back, from_ahead, one_out, three_out):
    one_out[:2] = (one[:2].astype(F32) + from_back[...].astype(F32)).astype(BF)
    one_out[2:] = one[2:]
    three_out[:2] = three[:2]
    three_out[2:] = (three[2:].astype(F32) + from_ahead[...].astype(F32)).astype(BF)


def fold_kernel(*refs):
    ins, outs = refs[:-RING], refs[-RING:]
    for k in range(RING):
        total = ins[0][k].astype(F32)
        for r in ins[1:]:
            total = total + r[k].astype(F32)
        outs[k][...] = total.astype(BF)


def act_kernel(*refs):
    gates, ups, pick_ref, out_ref = refs[:RING], refs[RING : 2 * RING], refs[-2], refs[-1]

    def total(parts):
        return functools.reduce(jnp.add, [part[...].astype(F32) for part in parts])

    gate, up = total(gates), total(ups)
    square = gate[320:322] + gate[322:324] + gate[324:326]
    inverse = lax.rsqrt(square / D + 1e-06)
    pick = pick_ref[...].astype(F32)
    factor = jnp.sum(pick[:, :128] * inverse[0:1] + pick[:, 128:] * inverse[1:2], 1, keepdims=True)
    act = (jax.nn.silu(gate[:ACT] * factor) * (up * factor)).astype(BF)
    for p in range(CHIPS):
        out_ref[p] = act


def down_kernel(act_ref, w_ref, s_ref, weight_ref, pick_ref, out_ref):
    pieces = []
    for e in range(EXP_DEV):
        rows = slice(e * 96, (e + 1) * 96)
        pieces.append(
            jnp.concatenate(
                [jnp.concatenate([act_ref[u * 2 + half, rows, :] for u in range(8)], 1) for half in range(2)], 0
            )
        )
    shared = jnp.concatenate(
        [jnp.concatenate([act_ref[u * 8 + t, 288:320, :] for u in range(2)], 1) for t in range(8)], 0
    )
    total = dot(s_ref[2], shared, NT)
    for e in range(EXP_DEV):
        weighted = (dot(w_ref[e], pieces[e], NT) * weight_ref[e]).astype(BF)
        total = total + dot(weighted, pick_ref[e])
    out_ref[...] = total.astype(out_ref.dtype)


def params(n=0, limit=24):
    size = limit * 1024 * 1024
    if n:
        return pltpu.CompilerParams(vmem_limit_bytes=size, dimension_semantics=("arbitrary",) * n)
    return pltpu.CompilerParams(vmem_limit_bytes=size)


def shape(*dims, dtype=BF):
    return jax.ShapeDtypeStruct(dims, dtype)


def whole(*dims):
    return pl.BlockSpec(dims, lambda *at: (0,) * len(dims))


def near_part(q, keys, w_uv):
    return pl.pallas_call(
        near_kernel,
        out_shape=(shape(ROWS, HD, dtype=F32), shape(4, 128, dtype=F32)),
        scratch_shapes=[pltpu.VMEM((ROWS, LAT), F32)],
        compiler_params=params(),
        name="near",
    )(q, keys, w_uv)


def vmem():
    return pl.BlockSpec(memory_space=pltpu.VMEM)


def far_cost():
    rows = SLOTS * ROWS
    return pl.CostEstimate(
        flops=2 * rows * 1024 * (WIDTH + LAT), bytes_accessed=24 * 1024 * 1024, transcendentals=rows * 1024
    )


def far_first(plan, prompt, sources, la, lb):
    return pl.pallas_call(
        functools.partial(far_first_kernel, plan),
        out_shape=(shape(SLOTS, ROWS, LAT), shape(SLOTS, 8, 128, dtype=F32)),
        in_specs=[pl.BlockSpec(memory_space=pltpu.SMEM)]
        + [vmem()] * len(sources)
        + [vmem(), vmem()],
        out_specs=(vmem(), vmem()),
        compiler_params=params(limit=18),
        cost_estimate=far_cost(),
        name="far_first",
    )(prompt, *sources, la, lb)


def far_second(plan, prompt, place, sources, la, lb, w_uv, early, early_stat):
    return pl.pallas_call(
        functools.partial(far_second_kernel, plan),
        out_shape=shape(CHIPS, MSG, HD),
        in_specs=[pl.BlockSpec(memory_space=pltpu.SMEM)] * 2
        + [vmem()] * len(sources)
        + [vmem(), vmem(), vmem(), pl.BlockSpec(memory_space=pl.ANY), vmem()],
        out_specs=pl.BlockSpec(memory_space=pltpu.HBM),
        scratch_shapes=[
            pltpu.VMEM((CHIPS, ROWS, LAT), BF),
            pltpu.VMEM((SLOTS, 8, 128), F32),
            pltpu.SemaphoreType.DMA,
            pltpu.VMEM((CHIPS, MSG, HD), BF),
            pltpu.SemaphoreType.DMA((HEADS // 4 + 1,)),
        ],
        compiler_params=params(limit=24),
        cost_estimate=far_cost(),
        name="far_second",
    )(prompt, place, *sources, la, lb, w_uv, early, early_stat)


def combine(received, near_out, near_stat):
    return pl.pallas_call(
        combine_kernel,
        out_shape=shape(CHIPS, DRAFT, HEADS * HD),
        compiler_params=params(),
        name="combine",
    )(received, near_out, near_stat)


def project(head, wm, wo):
    n, depth = wm.shape
    return pl.pallas_call(
        project_kernel,
        out_shape=shape(2 * n, head.shape[0]),
        in_specs=[pl.BlockSpec(memory_space=pltpu.HBM)] * 3,
        scratch_shapes=[
            pltpu.VMEM(head.shape, BF),
            pltpu.VMEM((2, n, depth), BF),
            pltpu.SemaphoreType.DMA((CUTS, 3)),
        ],
        compiler_params=params(),
        name="project",
    )(head, wm, wo)


def gate_up(at, own, rcv, pick, wm, wo, sm, so):
    n, half = wm.shape[2:]
    weights = pl.BlockSpec((2, 1, n, half), lambda e, c: (0, e, 0, 0))
    return pl.pallas_call(
        gate_up_kernel,
        out_shape=[shape(n, rows, 128) for rows in (GATE, UP) for n in PARTS],
        grid_spec=pltpu.PrefetchScalarGridSpec(
            num_scalar_prefetch=1,
            grid=(EXP_DEV,),
            in_specs=[
                whole(*own.shape),
                whole(*rcv.shape),
                pl.BlockSpec((1, CAP, 256), lambda e, c: (e, 0, 0)),
                weights,
                weights,
                whole(*sm.shape),
                whole(*so.shape),
            ],
            out_specs=[whole(n, rows, 128) for rows in (GATE, UP) for n in PARTS],
            scratch_shapes=[
                pltpu.VMEM((n, 256), BF),
                pltpu.VMEM((n, 256), BF),
                pltpu.VMEM((2, 256, 256), BF),
                pltpu.VMEM((2, CAP, half), BF),
            ],
        ),
        compiler_params=params(1),
        name="gate_up",
    )(at, own, rcv, pick, wm, wo, sm, so)


def pass_on(one, three, from_back, from_ahead):
    return pl.pallas_call(
        pass_on_kernel,
        out_shape=[shape(*one.shape)] * 2,
        compiler_params=params(),
        name="pass_on",
    )(one, three, from_back, from_ahead)


def fold(parts):
    return pl.pallas_call(
        fold_kernel,
        out_shape=[shape(*parts[0].shape[1:])] * RING,
        compiler_params=params(),
        name="fold",
    )(*parts)


def activate(gates, ups, pick):
    return pl.pallas_call(
        act_kernel,
        out_shape=shape(CHIPS, ACT, 128),
        compiler_params=params(),
        name="activate",
    )(*gates, *ups, pick)


def down(acts, w, s, weight, pick, dtype):
    n, half = w.shape[1:]
    return pl.pallas_call(
        down_kernel,
        out_shape=shape(n, 256, dtype=dtype),
        compiler_params=params(),
        cost_estimate=pl.CostEstimate(
            flops=2 * n * EXP_DEV * CAP * (half + 256), bytes_accessed=4 * 1024 * 1024, transcendentals=0
        ),
        name="down",
    )(acts, w, s, weight, pick)


def halves(value, core, axis):
    size = value.shape[axis] // 2
    mine = lax.dynamic_slice_in_dim(value, core * size, size, axis)
    other = lax.dynamic_slice_in_dim(value, (1 - core) * size, size, axis)
    return mine, other


def by_core(value):
    tail = value.shape[1:]
    return value.reshape(CHIPS, 2, DRAFT, *tail).swapaxes(0, 1).reshape(2 * CHIPS * DRAFT, *tail)


def turned(value):
    return jnp.concatenate([value[2:], value[:2]], 0)


def query_message(q):
    latent = q[:, :LAT].reshape(HALF, 4, 128).swapaxes(0, 1).reshape(4 * HALF, 128)
    rope = q[:, LAT:].reshape(2, HALF // 2, ROPE).swapaxes(0, 1).reshape(HALF // 2, 2 * ROPE)
    return jnp.concatenate([latent, rope], 0)


def per_device(
    queries,
    draft_latents,
    prefix_latents,
    prefix_of,
    accepted,
    w_uv,
    w_out,
    residual,
    norm_gain,
    w_gate_up,
    w_down,
    shared_gate_up,
    shared_down,
    expert_ids,
    expert_gates,
):
    pre = lax.axis_index("pre")
    core, chip = pre % 2, pre // 2
    z, x = chip // RING, chip % RING
    tokens = expert_ids.shape[0]

    q_own = queries[0].swapaxes(0, 1).reshape(ROWS, WIDTH)
    q_first = query_message(q_own[:HALF])
    q_second = query_message(q_own[HALF:])
    first_in = [lax.ppermute(q_first, "pre", X_BY[d]) for d in (1, 3)]
    second_in = [lax.ppermute(q_second, "pre", Z_BY[d]) for d in (1, 3)]
    latents = prefix_latents.swapaxes(1, 2)
    latents_other = swap_core(latents)
    first_in[0], q_first, q_second = lax.optimization_barrier((first_in[0], q_first, q_second))
    first_far = lax.ppermute(q_first, "pre", X_BY[2])
    second_far = lax.ppermute(q_second, "pre", Z_BY[2])
    first = jnp.stack([q_first, first_in[0], first_far, first_in[1]])
    second = jnp.stack([q_second, second_in[0], second_far, second_in[1]])
    first_1, first_3 = [lax.ppermute(first, "pre", Z_BY[d]) for d in (1, 3)]
    second_1, second_3 = [lax.ppermute(second, "pre", X_BY[d]) for d in (1, 3)]
    first_1, first_3, second_1, second_3, w_out = lax.optimization_barrier(
        (first_1, first_3, second_1, second_3, w_out.T)
    )
    w_out_o = swap_core(w_out)
    first_2 = lax.ppermute(turned(first_1), "pre", Z_BY[1])
    second_2 = lax.ppermute(turned(second_1), "pre", X_BY[1])
    sources = (first, first_1, first_3, second, second_1, second_3, first_2, second_2)
    early, late, early_plan, late_plan = [], [], [], []
    for dz, dx in NEAR_SPOTS + FAR_SPOTS:
        spots = tuple(
            (base + {0: 0, 1: 1, 3: 2}[slow], fast) if slow != 2 else (forwarded, (fast + 2) % RING)
            for base, forwarded, slow, fast in ((0, 6, dz, dx), (3, 7, dx, dz))
        )
        if len(early) < SLOTS:
            early.append((dz, dx))
            early_plan.append(spots)
        else:
            late.append((dz, dx))
            late_plan.append(spots)

    def chips_of(spots):
        back = jnp.array(spots, jnp.int32)
        return ((z - back[:, 0]) % RING) * RING + (x - back[:, 1]) % RING

    early_chip, late_chip = chips_of(early), chips_of(late)
    early_out, early_stat = far_first(
        early_plan, jnp.take(prefix_of, early_chip * 2 + core, axis=0), sources[:6], latents, latents_other
    )
    messages = far_second(
        late_plan,
        jnp.take(prefix_of, late_chip * 2 + core, axis=0),
        jnp.concatenate([early_chip, late_chip]),
        sources,
        latents,
        latents_other,
        w_uv,
        early_out,
        early_stat,
    )
    messages, w_gate_up, draft_latents = lax.optimization_barrier((messages, w_gate_up, draft_latents))
    received = chip_exchange(messages)
    pair_m, pair_send = halves(w_gate_up.transpose(2, 0, 1, 3), core, 3)
    near_keys = jnp.pad(draft_latents[0], ((0, 128 - DRAFT), (0, 0)))
    near_out, near_stat = near_part(q_own, near_keys, w_uv)

    received, near_out, pair_send = lax.optimization_barrier((received, near_out, pair_send))
    heads = combine(received, near_out, near_stat)
    held = (residual, norm_gain, w_down, shared_gate_up, shared_down, expert_ids, accepted, pair_send)
    heads, held = lax.optimization_barrier((heads, held))
    residual, norm_gain, w_down, shared_gate_up, shared_down, expert_ids, accepted, pair_send = held
    shared_m, shared_send = halves(shared_gate_up.swapaxes(0, 1), core, 2)
    down_m, down_send = halves(w_down.swapaxes(1, 2), core, 2)
    shared_down_m, shared_down_send = halves(shared_down.T, core, 1)
    token = jnp.arange(tokens, dtype=jnp.int32)
    order = by_core(token)
    to_order = (token[:, None] == order[None, :]).astype(BF)
    skip_m, skip_send = halves(dot(residual.T, to_order).astype(BF), core, 1)
    gain = jnp.broadcast_to(norm_gain[:, None], skip_m.shape)
    misc_m = jnp.concatenate([shared_m, shared_down_m[None], jnp.concatenate([skip_m, gain], 1)[None]], 0)
    misc_send = jnp.concatenate(
        [shared_send, shared_down_send[None], jnp.concatenate([skip_send, gain], 1)[None]], 0
    )
    live = by_core((jnp.arange(DRAFT)[None, :] < accepted[:, None]).reshape(tokens).astype(F32))
    local_experts = lax.axis_index("exp") * EXP_DEV + jnp.arange(EXP_DEV, dtype=jnp.int32)
    chosen = by_core(expert_ids)[:, :, None] == local_experts[None, None, :]
    routed = jnp.any(chosen, 1)
    weights = jnp.sum(jnp.where(chosen, by_core(expert_gates)[:, :, None], 0.0), 1) * live[:, None]
    position = jnp.cumsum(routed.astype(jnp.int32), 0) - 1
    slot_hit = routed.T[:, None, :] & (
        position.T[:, None, :] == jnp.arange(CAP, dtype=jnp.int32)[None, :, None]
    )
    pick = slot_hit.astype(BF)
    slot_weight = jnp.sum(jnp.where(slot_hit, weights.T[:, None, :], 0.0), 2)[:, None, :]
    my_slots = lax.dynamic_slice_in_dim(pick, (chip % 2) * 96, 96, 1).reshape(288, tokens)
    my_tokens = (token[None, :] == (chip % 8) * 32 + jnp.arange(32, dtype=jnp.int32)[:, None]).astype(BF)
    my_pick = jnp.concatenate([my_slots, my_tokens], 0)

    pair_o, down_o, misc_o = [swap_core(v) for v in (pair_send, down_send, misc_send)]
    at = jnp.stack([core, z, x]).astype(jnp.int32)
    head_in = chip_exchange(heads)
    head_in, pair_o, down_o, misc_o, misc_m, pick, my_pick, slot_weight, at = lax.optimization_barrier(
        (head_in, pair_o, down_o, misc_o, misc_m, pick, my_pick, slot_weight, at)
    )
    head_out = head_in.reshape(CHIPS * DRAFT, HEADS * HD)
    skip = jnp.concatenate([misc_m[3, :, :128], misc_o[3, :, :128]], 0)
    hidden = skip.astype(F32) + exp_sum(project(head_out, w_out, w_out_o))
    hidden_rcv = swap_core(hidden)

    parts = gate_up(at, hidden, hidden_rcv, pick, pair_m, pair_o, misc_m, misc_o)
    gates, ups = parts[:5], parts[5:]
    gates_in = [lax.ppermute(gates[3], "pre", X_BY[1]), lax.ppermute(gates[4], "pre", X_BY[3])]
    ups_in = [lax.ppermute(ups[3], "pre", Z_BY[1]), lax.ppermute(ups[4], "pre", Z_BY[3])]
    gates_on = pass_on(gates[1], gates[2], *gates_in)
    ups_on = pass_on(ups[1], ups[2], *ups_in)
    gates_in = [lax.ppermute(gates_on[0], "pre", X_BY[1]), lax.ppermute(gates_on[1], "pre", X_BY[3])]
    ups_in = [lax.ppermute(ups_on[0], "pre", Z_BY[1]), lax.ppermute(ups_on[1], "pre", Z_BY[3])]
    gates = fold([gates[0]] + gates_in)
    ups = fold([ups[0]] + ups_in)
    gates_in = [lax.ppermute(gates[d], "pre", Z_BY[d]) for d in (1, 3, 2)]
    ups_in = [lax.ppermute(ups[d], "pre", X_BY[d]) for d in (1, 3, 2)]
    acts = activate([gates[0]] + gates_in, [ups[0]] + ups_in, my_pick)
    acts = chip_exchange(acts)
    other = swap_core(down(acts, down_o, misc_o, slot_weight, pick, BF))
    mine = down(acts, down_m, misc_m, slot_weight, pick, F32)
    mixed = exp_sum((mine + other.astype(F32)).astype(BF))

    n = mine.shape[0]
    kept, other_half = hidden[:n], hidden_rcv[n:]
    hidden_m = jnp.where(
        core == 0, jnp.concatenate([kept, other_half], 1), jnp.concatenate([other_half, kept], 1)
    )
    return dot((hidden_m + mixed).astype(BF), to_order, NT).astype(BF).T


def solution(mesh):
    return jax.shard_map(
        per_device,
        mesh=mesh,
        in_specs=(
            P("pre", None, "exp", None),
            P("pre", None, None),
            P(None, "pre", None),
            P(),
            P(),
            P("exp", None, None),
            P("exp", "pre"),
            P(None, "pre"),
            P("pre"),
            P("exp", "pre", None, None),
            P("exp", None, "pre"),
            P("pre", None, "exp"),
            P("exp", "pre"),
            P(),
            P(),
        ),
        out_specs=P(None, "pre"),
        check_vma=False,
    )
```

```python
import functools
import math

import jax
import jax.numpy as jnp
from jax import lax
from jax.experimental import pallas as pl
from jax.experimental.pallas import tpu as pltpu
from jax.sharding import PartitionSpec as P

D = 7168
LAT = 512
ROPE = 64
HD = 128
DRAFT = 8
EXP_DEV = 3
CAP = 192
RING = 4
CHIPS = 16
HEADS = 32
ROWS = HEADS * DRAFT
MSG = ROWS + 16
HALF = ROWS // 2
WIDTH = LAT + ROPE
QROWS = HALF * WIDTH // 128
GATE = 336
PARTS = (4, 4, 4, 2, 2)
UP = 320
ACT = 320
KEXP = (HD + ROPE) ** (-0.5) * math.log2(math.e)
BF = jnp.bfloat16
F32 = jnp.float32


def device_of(z, x, c):
    return (z * RING + x) * 2 + c


def pre_pairs(move):
    return [
        (device_of(z, x, c), device_of(*move(z, x, c)))
        for z in range(RING)
        for x in range(RING)
        for c in range(2)
    ]


CORE = pre_pairs(lambda z, x, c: (z, x, 1 - c))
X_BY = {d: pre_pairs(lambda z, x, c: (z, (x + d) % RING, c)) for d in (1, 2, 3)}
Z_BY = {d: pre_pairs(lambda z, x, c: ((z + d) % RING, x, c)) for d in (1, 2, 3)}
Y_BY = {d: [(e, (e + d) % RING) for e in range(RING)] for d in (1, 2, 3)}
NEAR_SPOTS = [(0, 0)] + [(dz, dx) for dz in (0, 1, 3) for dx in (0, 1, 3) if dz or dx]
FAR_SPOTS = [(dz, dx) for dz in range(RING) for dx in range(RING) if 2 in (dz, dx)]
SAME_CORE = [[chip * 2 + c for chip in range(CHIPS)] for c in range(2)]


def swap_core(value):
    return lax.ppermute(value, "pre", CORE)


def ring_send(values, pairs):
    return [lax.ppermute(value, "pre", pairs[d]) for d, value in zip((1, 2, 3), values)]


def exp_sum(value):
    others = {d: lax.ppermute(value, "exp", Y_BY[d]).astype(F32) for d in (2, 1, 3)}
    return (value.astype(F32) + others[2]) + (others[1] + others[3])


def chip_exchange(value):
    return lax.all_to_all(value, "pre", 0, 0, axis_index_groups=SAME_CORE)


def dot(a, b, dims=((1,), (0,))):
    return lax.dot_general(a, b, (dims, ((), ())), preferred_element_type=F32)


NT = ((1,), (1,))


def eye(n):
    return lax.broadcasted_iota(jnp.int32, (n, n), 0) == lax.broadcasted_iota(jnp.int32, (n, n), 1)


def column_to_rows(column):
    mask = eye(128)
    parts = [
        jnp.sum(jnp.where(mask, jnp.broadcast_to(column[b * 128 : (b + 1) * 128], (128, 128)), 0.0), 0, keepdims=True)
        for b in range(column.shape[0] // 128)
    ]
    return jnp.concatenate(parts, 0)


def three_terms(rows):
    high = rows.astype(BF).astype(F32)
    rest = rows - high
    mid = rest.astype(BF).astype(F32)
    return [high, mid, rest - mid]


def near_kernel(q_ref, k_ref, w_ref, out_ref, stat_ref, acc):
    keys = k_ref[...]
    scores = dot(q_ref[...], keys, NT)
    draft = lax.broadcasted_iota(jnp.int32, scores.shape, 0) % DRAFT
    key = lax.broadcasted_iota(jnp.int32, scores.shape, 1)
    allowed = key <= draft
    top = jnp.max(jnp.where(allowed, scores, -jnp.inf), 1, keepdims=True)
    weight = jnp.where(allowed, jnp.exp2((scores - top) * KEXP), 0.0).astype(BF)
    total = jnp.sum(weight.astype(F32), 1, keepdims=True)
    acc[...] = dot(weight, keys[:, :LAT])
    stat_ref[...] = jnp.concatenate([column_to_rows(top), column_to_rows(total)], 0)
    for h in range(HEADS):
        rows = slice(h * DRAFT, (h + 1) * DRAFT)
        out_ref[rows, :] = dot(acc[rows, :].astype(BF), w_ref[h])


SLOTS = CHIPS // 2


def attend(q_refs, la_ref, lb_ref, out_ref, stat_ref):
    parts = []
    for b in range(4):
        rows = slice(b * HALF, (b + 1) * HALF)
        parts.append(jnp.concatenate([q[rows, :] for q in q_refs], 0))
    ropes = [q[4 * HALF : QROWS, :] for q in q_refs]
    parts.append(jnp.concatenate([r[:, s : s + ROPE] for r in ropes for s in (0, ROPE)], 0))
    q = jnp.concatenate(parts, 1)
    sa = dot(q, la_ref[...])
    sb = dot(q, lb_ref[...])
    top = jnp.max(jnp.maximum(sa, sb), 1, keepdims=True)
    wa = jnp.exp2((sa - top) * KEXP).astype(BF)
    wb = jnp.exp2((sb - top) * KEXP).astype(BF)
    total = jnp.sum(wa.astype(F32) + wb.astype(F32), 1, keepdims=True)
    out_ref[...] = (dot(wa, la_ref[:LAT], NT) + dot(wb, lb_ref[:LAT], NT)).astype(BF)
    stat_ref[...] = jnp.concatenate(
        [column_to_rows(top), column_to_rows(total), jnp.zeros((4, 128), F32)], 0
    )


def attend_all(plan, prompt, sources, la_ref, lb_ref, out_ref, stat_ref):
    for n, spots in enumerate(plan):
        which = prompt[n]
        q_refs = [sources[source].at[at] for source, at in spots]
        attend(q_refs, la_ref.at[which], lb_ref.at[which], out_ref.at[n], stat_ref.at[n])


def far_first_kernel(plan, prompt, *refs):
    attend_all(plan, prompt, refs[:-4], *refs[-4:])


def far_second_kernel(plan, prompt, place, *refs):
    sources = refs[:-11]
    la_ref, lb_ref, w_ref, early_ref, early_stat, out_ref, acc, stat, early_sem, msg_ref, sems = refs[-11:]
    fetch = pltpu.make_async_copy(early_ref, acc.at[pl.ds(0, SLOTS)], early_sem)
    fetch.start()
    attend_all(plan, prompt, sources, la_ref, lb_ref, acc.at[pl.ds(SLOTS, SLOTS)], stat)
    fetch.wait()
    for n in range(CHIPS):
        rows = early_stat[n] if n < SLOTS else stat[n - SLOTS]
        extra = three_terms(rows[0:2]) + three_terms(rows[2:4]) + [jnp.zeros((4, 128), F32)]
        msg_ref[place[n], ROWS:MSG, :] = jnp.concatenate(extra, 0).astype(BF)
    def send(start, rows, sem):
        part = pl.ds(start, rows)
        return pltpu.make_async_copy(msg_ref.at[:, part, :], out_ref.at[:, part, :], sem)

    send(ROWS, 16, sems.at[HEADS // 4]).start()
    low = lax.broadcasted_iota(jnp.int32, (CHIPS * 16, HD), 0) % 16 < DRAFT

    @pl.loop(0, HEADS // 4)
    def _(quad):
        for r in range(2):
            pair = quad * 2 + r
            start = pl.multiple_of(pair * 16, 16)
            rows = acc[:, pl.ds(start, 16), :].reshape(CHIPS * 16, LAT)
            both = dot(rows, jnp.concatenate([w_ref[pair * 2], w_ref[pair * 2 + 1]], 1))
            picked = jnp.where(low, both[:, :HD], both[:, HD:]).astype(BF)
            for n in range(CHIPS):
                msg_ref[place[n], pl.ds(start, 16), :] = picked[n * 16 : (n + 1) * 16]
        send(pl.multiple_of(quad * 32, 32), 32, sems.at[quad]).start()

    send(ROWS, 16, sems.at[HEADS // 4]).wait()

    @pl.loop(0, HEADS // 4)
    def _(quad):
        send(pl.multiple_of(quad * 32, 32), 32, sems.at[quad]).wait()


def combine_kernel(rec_ref, near_ref, stat_ref, out_ref):
    tops, totals = [], []
    for p in range(CHIPS):
        extra = rec_ref[p, ROWS:MSG, :].astype(F32)
        tops.append(extra[0:2] + extra[2:4] + extra[4:6])
        totals.append(extra[6:8] + extra[8:10] + extra[10:12])
    tops.append(stat_ref[0:2])
    totals.append(stat_ref[2:4])
    best = functools.reduce(jnp.maximum, tops)
    scale = [jnp.exp2((t - best) * KEXP) for t in tops]
    whole = functools.reduce(jnp.add, [s * t for s, t in zip(scale, totals)])
    scale = [s / whole for s in scale]
    blocks = []
    for b in range(2):
        table = jnp.concatenate(
            [s[b : b + 1] for s in scale] + [jnp.zeros((128 - len(scale), 128), F32)], 0
        ).T
        rows = slice(b * 128, (b + 1) * 128)
        value = near_ref[rows, :] * table[:, CHIPS : CHIPS + 1]
        for p in range(CHIPS):
            value = value + rec_ref[p, rows, :].astype(F32) * table[:, p : p + 1]
        blocks.append(value)
    value = jnp.concatenate(blocks, 0)
    flat = jnp.concatenate([value[h * DRAFT : (h + 1) * DRAFT] for h in range(HEADS)], 1).astype(BF)
    for p in range(CHIPS):
        out_ref[p] = flat


CUTS = 4


def project_kernel(head_ref, wm_ref, wo_ref, out_ref, head, weight, sems):
    step = head.shape[1] // CUTS
    copies = []
    for c in range(CUTS):
        part = pl.ds(c * step, step)
        copies.append(
            [
                pltpu.make_async_copy(head_ref.at[:, part], head.at[:, part], sems.at[c, 0]),
                pltpu.make_async_copy(wm_ref.at[:, part], weight.at[0, :, part], sems.at[c, 1]),
                pltpu.make_async_copy(wo_ref.at[:, part], weight.at[1, :, part], sems.at[c, 2]),
            ]
        )
    for group in copies:
        for copy in group:
            copy.start()
    totals = [0.0, 0.0]
    for c, group in enumerate(copies):
        for copy in group:
            copy.wait()
        part = slice(c * step, (c + 1) * step)
        totals = [t + dot(weight[k, :, part], head[:, part], NT) for k, t in enumerate(totals)]
    out_ref[...] = jnp.concatenate(totals, 0).astype(BF)


def gate_up_kernel(
    at_ref, own_ref, rcv_ref, pick_ref, wm_ref, wo_ref, sm_ref, so_ref, *refs
):
    outs, (xm, xo, pair, wide) = refs[:10], refs[10:]
    e = pl.program_id(0)
    core, z, x = at_ref[0], at_ref[1], at_ref[2]
    n = xm.shape[0]

    def spot(group, slow, fast):
        if slow == 2:
            return group[3 + fast // 2].at[fast % 2]
        return group[{0: 0, 1: 1, 3: 2}[slow]].at[fast]

    def destinations():
        for dx in range(RING):
            for dz in range(RING):
                chip = lax.rem(z + dz, RING) * RING + lax.rem(x + dx, RING)
                yield (spot(outs[:5], dx, dz), spot(outs[5:], dz, dx)), chip

    @pl.when(e == 0)
    def _():
        square = jnp.zeros((1, 256), F32)
        for keep, misc_ref, mine, theirs in ((xm, sm_ref, 0, n), (xo, so_ref, n, 0)):
            own = own_ref[mine : mine + n, :]
            rcv = rcv_ref[theirs : theirs + n, :]
            whole = jnp.concatenate([jnp.where(core == 0, own, rcv), jnp.where(core == 0, rcv, own)], 1)
            square = square + jnp.sum(whole * whole, 0, keepdims=True)
            keep[...] = (whole * misc_ref[3][:, 128:129].astype(F32)).astype(BF)
        terms = three_terms(jnp.concatenate([square[:, :128], square[:, 128:]], 0))
        rows = jnp.concatenate(terms + [jnp.zeros((10, 128), F32)], 0).astype(BF)
        same = eye(256).astype(BF)
        all_m = dot(same, xm[...], NT).astype(BF)
        all_o = dot(same, xo[...], NT).astype(BF)
        for g in range(2):
            pair[g] = (dot(all_m, sm_ref[g]) + dot(all_o, so_ref[g])).astype(BF)
        for pieces, chip in destinations():
            pieces[0][320:336, :] = rows
            top = pl.multiple_of(lax.rem(chip, 8) * 32, 32)
            left = pl.multiple_of(lax.div(chip, 8) * 128, 128)
            for g in range(2):
                pieces[g][288:320, :] = pair[g, pl.ds(top, 32), pl.ds(left, 128)]

    picked_m = dot(pick_ref[0], xm[...], NT).astype(BF)
    picked_o = dot(pick_ref[0], xo[...], NT).astype(BF)
    for g in range(2):
        wide[g] = (dot(picked_m, wm_ref[g, 0]) + dot(picked_o, wo_ref[g, 0])).astype(BF)
    start = pl.multiple_of(e * 96, 32)
    for pieces, chip in destinations():
        top = pl.multiple_of(lax.rem(chip, 2) * 96, 32)
        left = pl.multiple_of(lax.div(chip, 2) * 128, 128)
        for g in range(2):
            pieces[g][pl.ds(start, 96), :] = wide[g, pl.ds(top, 96), pl.ds(left, 128)]


def pass_on_kernel(one, three, from_back, from_ahead, one_out, three_out):
    one_out[:2] = (one[:2].astype(F32) + from_back[...].astype(F32)).astype(BF)
    one_out[2:] = one[2:]
    three_out[:2] = three[:2]
    three_out[2:] = (three[2:].astype(F32) + from_ahead[...].astype(F32)).astype(BF)


def fold_kernel(*refs):
    ins, outs = refs[:-RING], refs[-RING:]
    for k in range(RING):
        total = ins[0][k].astype(F32)
        for r in ins[1:]:
            total = total + r[k].astype(F32)
        outs[k][...] = total.astype(BF)


def act_kernel(*refs):
    gates, ups, pick_ref, out_ref = refs[:RING], refs[RING : 2 * RING], refs[-2], refs[-1]

    def total(parts):
        return functools.reduce(jnp.add, [part[...].astype(F32) for part in parts])

    gate, up = total(gates), total(ups)
    square = gate[320:322] + gate[322:324] + gate[324:326]
    inverse = lax.rsqrt(square / D + 1e-06)
    pick = pick_ref[...].astype(F32)
    factor = jnp.sum(pick[:, :128] * inverse[0:1] + pick[:, 128:] * inverse[1:2], 1, keepdims=True)
    act = (jax.nn.silu(gate[:ACT] * factor) * (up * factor)).astype(BF)
    for p in range(CHIPS):
        out_ref[p] = act


def down_kernel(act_ref, w_ref, s_ref, weight_ref, pick_ref, out_ref):
    pieces = []
    for e in range(EXP_DEV):
        rows = slice(e * 96, (e + 1) * 96)
        pieces.append(
            jnp.concatenate(
                [jnp.concatenate([act_ref[u * 2 + half, rows, :] for u in range(8)], 1) for half in range(2)], 0
            )
        )
    shared = jnp.concatenate(
        [jnp.concatenate([act_ref[u * 8 + t, 288:320, :] for u in range(2)], 1) for t in range(8)], 0
    )
    total = dot(s_ref[2], shared, NT)
    for e in range(EXP_DEV):
        weighted = (dot(w_ref[e], pieces[e], NT) * weight_ref[e]).astype(BF)
        total = total + dot(weighted, pick_ref[e])
    out_ref[...] = total.astype(out_ref.dtype)


def params(n=0, limit=24):
    size = limit * 1024 * 1024
    if n:
        return pltpu.CompilerParams(vmem_limit_bytes=size, dimension_semantics=("arbitrary",) * n)
    return pltpu.CompilerParams(vmem_limit_bytes=size)


def shape(*dims, dtype=BF):
    return jax.ShapeDtypeStruct(dims, dtype)


def whole(*dims):
    return pl.BlockSpec(dims, lambda *at: (0,) * len(dims))


def near_part(q, keys, w_uv):
    return pl.pallas_call(
        near_kernel,
        out_shape=(shape(ROWS, HD, dtype=F32), shape(4, 128, dtype=F32)),
        scratch_shapes=[pltpu.VMEM((ROWS, LAT), F32)],
        compiler_params=params(),
        name="near",
    )(q, keys, w_uv)


def vmem():
    return pl.BlockSpec(memory_space=pltpu.VMEM)


def far_cost():
    rows = SLOTS * ROWS
    return pl.CostEstimate(
        flops=2 * rows * 1024 * (WIDTH + LAT), bytes_accessed=24 * 1024 * 1024, transcendentals=rows * 1024
    )


def far_first(plan, prompt, sources, la, lb):
    return pl.pallas_call(
        functools.partial(far_first_kernel, plan),
        out_shape=(shape(SLOTS, ROWS, LAT), shape(SLOTS, 8, 128, dtype=F32)),
        in_specs=[pl.BlockSpec(memory_space=pltpu.SMEM)]
        + [vmem()] * len(sources)
        + [vmem(), vmem()],
        out_specs=(vmem(), vmem()),
        compiler_params=params(limit=18),
        cost_estimate=far_cost(),
        name="far_first",
    )(prompt, *sources, la, lb)


def far_second(plan, prompt, place, sources, la, lb, w_uv, early, early_stat):
    return pl.pallas_call(
        functools.partial(far_second_kernel, plan),
        out_shape=shape(CHIPS, MSG, HD),
        in_specs=[pl.BlockSpec(memory_space=pltpu.SMEM)] * 2
        + [vmem()] * len(sources)
        + [vmem(), vmem(), vmem(), pl.BlockSpec(memory_space=pl.ANY), vmem()],
        out_specs=pl.BlockSpec(memory_space=pltpu.HBM),
        scratch_shapes=[
            pltpu.VMEM((CHIPS, ROWS, LAT), BF),
            pltpu.VMEM((SLOTS, 8, 128), F32),
            pltpu.SemaphoreType.DMA,
            pltpu.VMEM((CHIPS, MSG, HD), BF),
            pltpu.SemaphoreType.DMA((HEADS // 4 + 1,)),
        ],
        compiler_params=params(limit=24),
        cost_estimate=far_cost(),
        name="far_second",
    )(prompt, place, *sources, la, lb, w_uv, early, early_stat)


def combine(received, near_out, near_stat):
    return pl.pallas_call(
        combine_kernel,
        out_shape=shape(CHIPS, DRAFT, HEADS * HD),
        compiler_params=params(),
        name="combine",
    )(received, near_out, near_stat)


def project(head, wm, wo):
    n, depth = wm.shape
    return pl.pallas_call(
        project_kernel,
        out_shape=shape(2 * n, head.shape[0]),
        in_specs=[pl.BlockSpec(memory_space=pltpu.HBM)] * 3,
        scratch_shapes=[
            pltpu.VMEM(head.shape, BF),
            pltpu.VMEM((2, n, depth), BF),
            pltpu.SemaphoreType.DMA((CUTS, 3)),
        ],
        compiler_params=params(),
        name="project",
    )(head, wm, wo)


def gate_up(at, own, rcv, pick, wm, wo, sm, so):
    n, half = wm.shape[2:]
    weights = pl.BlockSpec((2, 1, n, half), lambda e, c: (0, e, 0, 0))
    return pl.pallas_call(
        gate_up_kernel,
        out_shape=[shape(n, rows, 128) for rows in (GATE, UP) for n in PARTS],
        grid_spec=pltpu.PrefetchScalarGridSpec(
            num_scalar_prefetch=1,
            grid=(EXP_DEV,),
            in_specs=[
                whole(*own.shape),
                whole(*rcv.shape),
                pl.BlockSpec((1, CAP, 256), lambda e, c: (e, 0, 0)),
                weights,
                weights,
                whole(*sm.shape),
                whole(*so.shape),
            ],
            out_specs=[whole(n, rows, 128) for rows in (GATE, UP) for n in PARTS],
            scratch_shapes=[
                pltpu.VMEM((n, 256), BF),
                pltpu.VMEM((n, 256), BF),
                pltpu.VMEM((2, 256, 256), BF),
                pltpu.VMEM((2, CAP, half), BF),
            ],
        ),
        compiler_params=params(1),
        name="gate_up",
    )(at, own, rcv, pick, wm, wo, sm, so)


def pass_on(one, three, from_back, from_ahead):
    return pl.pallas_call(
        pass_on_kernel,
        out_shape=[shape(*one.shape)] * 2,
        compiler_params=params(),
        name="pass_on",
    )(one, three, from_back, from_ahead)


def fold(parts):
    return pl.pallas_call(
        fold_kernel,
        out_shape=[shape(*parts[0].shape[1:])] * RING,
        compiler_params=params(),
        name="fold",
    )(*parts)


def activate(gates, ups, pick):
    return pl.pallas_call(
        act_kernel,
        out_shape=shape(CHIPS, ACT, 128),
        compiler_params=params(),
        name="activate",
    )(*gates, *ups, pick)


def down(acts, w, s, weight, pick, dtype):
    n, half = w.shape[1:]
    return pl.pallas_call(
        down_kernel,
        out_shape=shape(n, 256, dtype=dtype),
        compiler_params=params(),
        cost_estimate=pl.CostEstimate(
            flops=2 * n * EXP_DEV * CAP * (half + 256), bytes_accessed=4 * 1024 * 1024, transcendentals=0
        ),
        name="down",
    )(acts, w, s, weight, pick)


def halves(value, core, axis):
    size = value.shape[axis] // 2
    mine = lax.dynamic_slice_in_dim(value, core * size, size, axis)
    other = lax.dynamic_slice_in_dim(value, (1 - core) * size, size, axis)
    return mine, other


def by_core(value):
    tail = value.shape[1:]
    return value.reshape(CHIPS, 2, DRAFT, *tail).swapaxes(0, 1).reshape(2 * CHIPS * DRAFT, *tail)


def turned(value):
    return jnp.concatenate([value[2:], value[:2]], 0)


def query_message(q):
    latent = q[:, :LAT].reshape(HALF, 4, 128).swapaxes(0, 1).reshape(4 * HALF, 128)
    rope = q[:, LAT:].reshape(2, HALF // 2, ROPE).swapaxes(0, 1).reshape(HALF // 2, 2 * ROPE)
    return jnp.concatenate([latent, rope], 0)


def per_device(
    queries,
    draft_latents,
    prefix_latents,
    prefix_of,
    accepted,
    w_uv,
    w_out,
    residual,
    norm_gain,
    w_gate_up,
    w_down,
    shared_gate_up,
    shared_down,
    expert_ids,
    expert_gates,
):
    pre = lax.axis_index("pre")
    core, chip = pre % 2, pre // 2
    z, x = chip // RING, chip % RING
    tokens = expert_ids.shape[0]

    q_own = queries[0].swapaxes(0, 1).reshape(ROWS, WIDTH)
    q_first = query_message(q_own[:HALF])
    q_second = query_message(q_own[HALF:])
    first_in = [lax.ppermute(q_first, "pre", X_BY[d]) for d in (1, 3)]
    second_in = [lax.ppermute(q_second, "pre", Z_BY[d]) for d in (1, 3)]
    latents = prefix_latents.swapaxes(1, 2)
    latents_other = swap_core(latents)
    first_in[0], q_first, q_second = lax.optimization_barrier((first_in[0], q_first, q_second))
    first_far = lax.ppermute(q_first, "pre", X_BY[2])
    second_far = lax.ppermute(q_second, "pre", Z_BY[2])
    first = jnp.stack([q_first, first_in[0], first_far, first_in[1]])
    second = jnp.stack([q_second, second_in[0], second_far, second_in[1]])
    first_1, first_3 = [lax.ppermute(first, "pre", Z_BY[d]) for d in (1, 3)]
    second_1, second_3 = [lax.ppermute(second, "pre", X_BY[d]) for d in (1, 3)]
    second_1, w_out = lax.optimization_barrier((second_1, w_out.T))
    w_out_o = swap_core(w_out)
    first_2 = lax.ppermute(turned(first_1), "pre", Z_BY[1])
    second_2 = lax.ppermute(turned(second_1), "pre", X_BY[1])
    sources = (first, first_1, first_3, second, second_1, second_3, first_2, second_2)
    early, late, early_plan, late_plan = [], [], [], []
    for dz, dx in NEAR_SPOTS + FAR_SPOTS:
        spots = tuple(
            (base + {0: 0, 1: 1, 3: 2}[slow], fast) if slow != 2 else (forwarded, (fast + 2) % RING)
            for base, forwarded, slow, fast in ((0, 6, dz, dx), (3, 7, dx, dz))
        )
        if len(early) < SLOTS:
            early.append((dz, dx))
            early_plan.append(spots)
        else:
            late.append((dz, dx))
            late_plan.append(spots)

    def chips_of(spots):
        back = jnp.array(spots, jnp.int32)
        return ((z - back[:, 0]) % RING) * RING + (x - back[:, 1]) % RING

    early_chip, late_chip = chips_of(early), chips_of(late)
    early_out, early_stat = far_first(
        early_plan, jnp.take(prefix_of, early_chip * 2 + core, axis=0), sources[:6], latents, latents_other
    )
    messages = far_second(
        late_plan,
        jnp.take(prefix_of, late_chip * 2 + core, axis=0),
        jnp.concatenate([early_chip, late_chip]),
        sources,
        latents,
        latents_other,
        w_uv,
        early_out,
        early_stat,
    )
    messages, w_gate_up, draft_latents = lax.optimization_barrier((messages, w_gate_up, draft_latents))
    received = chip_exchange(messages)
    pair_m, pair_send = halves(w_gate_up.transpose(2, 0, 1, 3), core, 3)
    near_keys = jnp.pad(draft_latents[0], ((0, 128 - DRAFT), (0, 0)))
    near_out, near_stat = near_part(q_own, near_keys, w_uv)

    received, near_out, pair_send = lax.optimization_barrier((received, near_out, pair_send))
    heads = combine(received, near_out, near_stat)
    held = (residual, norm_gain, w_down, shared_gate_up, shared_down, expert_ids, accepted, pair_send)
    heads, held = lax.optimization_barrier((heads, held))
    residual, norm_gain, w_down, shared_gate_up, shared_down, expert_ids, accepted, pair_send = held
    shared_m, shared_send = halves(shared_gate_up.swapaxes(0, 1), core, 2)
    down_m, down_send = halves(w_down.swapaxes(1, 2), core, 2)
    shared_down_m, shared_down_send = halves(shared_down.T, core, 1)
    token = jnp.arange(tokens, dtype=jnp.int32)
    order = by_core(token)
    to_order = (token[:, None] == order[None, :]).astype(BF)
    skip_m, skip_send = halves(dot(residual.T, to_order).astype(BF), core, 1)
    gain = jnp.broadcast_to(norm_gain[:, None], skip_m.shape)
    misc_m = jnp.concatenate([shared_m, shared_down_m[None], jnp.concatenate([skip_m, gain], 1)[None]], 0)
    misc_send = jnp.concatenate(
        [shared_send, shared_down_send[None], jnp.concatenate([skip_send, gain], 1)[None]], 0
    )
    live = by_core((jnp.arange(DRAFT)[None, :] < accepted[:, None]).reshape(tokens).astype(F32))
    local_experts = lax.axis_index("exp") * EXP_DEV + jnp.arange(EXP_DEV, dtype=jnp.int32)
    chosen = by_core(expert_ids)[:, :, None] == local_experts[None, None, :]
    routed = jnp.any(chosen, 1)
    weights = jnp.sum(jnp.where(chosen, by_core(expert_gates)[:, :, None], 0.0), 1) * live[:, None]
    position = jnp.cumsum(routed.astype(jnp.int32), 0) - 1
    slot_hit = routed.T[:, None, :] & (
        position.T[:, None, :] == jnp.arange(CAP, dtype=jnp.int32)[None, :, None]
    )
    pick = slot_hit.astype(BF)
    slot_weight = jnp.sum(jnp.where(slot_hit, weights.T[:, None, :], 0.0), 2)[:, None, :]
    my_slots = lax.dynamic_slice_in_dim(pick, (chip % 2) * 96, 96, 1).reshape(288, tokens)
    my_tokens = (token[None, :] == (chip % 8) * 32 + jnp.arange(32, dtype=jnp.int32)[:, None]).astype(BF)
    my_pick = jnp.concatenate([my_slots, my_tokens], 0)

    pair_o, down_o, misc_o = [swap_core(v) for v in (pair_send, down_send, misc_send)]
    at = jnp.stack([core, z, x]).astype(jnp.int32)
    head_in = chip_exchange(heads)
    head_in, pair_o, down_o, misc_o, misc_m, pick, my_pick, slot_weight, at = lax.optimization_barrier(
        (head_in, pair_o, down_o, misc_o, misc_m, pick, my_pick, slot_weight, at)
    )
    head_out = head_in.reshape(CHIPS * DRAFT, HEADS * HD)
    skip = jnp.concatenate([misc_m[3, :, :128], misc_o[3, :, :128]], 0)
    hidden = skip.astype(F32) + exp_sum(project(head_out, w_out, w_out_o))
    hidden_rcv = swap_core(hidden)

    parts = gate_up(at, hidden, hidden_rcv, pick, pair_m, pair_o, misc_m, misc_o)
    gates, ups = parts[:5], parts[5:]
    gates_in = [lax.ppermute(gates[3], "pre", X_BY[1]), lax.ppermute(gates[4], "pre", X_BY[3])]
    ups_in = [lax.ppermute(ups[3], "pre", Z_BY[1]), lax.ppermute(ups[4], "pre", Z_BY[3])]
    gates_on = pass_on(gates[1], gates[2], *gates_in)
    ups_on = pass_on(ups[1], ups[2], *ups_in)
    gates_in = [lax.ppermute(gates_on[0], "pre", X_BY[1]), lax.ppermute(gates_on[1], "pre", X_BY[3])]
    ups_in = [lax.ppermute(ups_on[0], "pre", Z_BY[1]), lax.ppermute(ups_on[1], "pre", Z_BY[3])]
    gates = fold([gates[0]] + gates_in)
    ups = fold([ups[0]] + ups_in)
    gates_in = [lax.ppermute(gates[d], "pre", Z_BY[d]) for d in (1, 3, 2)]
    ups_in = [lax.ppermute(ups[d], "pre", X_BY[d]) for d in (1, 3, 2)]
    acts = activate([gates[0]] + gates_in, [ups[0]] + ups_in, my_pick)
    acts = chip_exchange(acts)
    other = swap_core(down(acts, down_o, misc_o, slot_weight, pick, BF))
    mine = down(acts, down_m, misc_m, slot_weight, pick, F32)
    mixed = exp_sum((mine + other.astype(F32)).astype(BF))

    n = mine.shape[0]
    kept, other_half = hidden[:n], hidden_rcv[n:]
    hidden_m = jnp.where(
        core == 0, jnp.concatenate([kept, other_half], 1), jnp.concatenate([other_half, kept], 1)
    )
    return dot((hidden_m + mixed).astype(BF), to_order, NT).astype(BF).T


def solution(mesh):
    return jax.shard_map(
        per_device,
        mesh=mesh,
        in_specs=(
            P("pre", None, "exp", None),
            P("pre", None, None),
            P(None, "pre", None),
            P(),
            P(),
            P("exp", None, None),
            P("exp", "pre"),
            P(None, "pre"),
            P("pre"),
            P("exp", "pre", None, None),
            P("exp", None, "pre"),
            P("pre", None, "exp"),
            P("exp", "pre"),
            P(),
            P(),
        ),
        out_specs=P(None, "pre"),
        check_vma=False,
    )
```
